256 devices in a mesh: ep: 64 (over z, y, core), tp: 4 (over x).
Axes of the slice: x: 4, y: 4, z: 8, core: 2. Of those that a mesh axis runs over, the one named last changes fastest.
Arguments:
- hidden_rows: bfloat16 [4096, 7168], P('ep', 'tp'), may hold values from -6 to 6
- expert_ids: int32 [4096, 8], P('ep'), may hold values from 0 to 63, all different within a row; in each aligned block of 64 rows (0 to 63, 64 to 127, ...) at most 12 rows name the same one
- affinity: float32 [4096, 8], P('ep'), may hold values from 0.05 to 1
- w_gate: bfloat16 [64, 7168, 1024], P('ep', None, 'tp'), may hold values from -0.0625 to 0.0625
- w_up: bfloat16 [64, 7168, 1024], P('ep', None, 'tp'), may hold values from -0.0625 to 0.0625
- w_down: bfloat16 [64, 1024, 7168], P('ep', 'tp'), may hold values from -0.1875 to 0.1875
Outputs:
- mixed_rows: bfloat16 [4096, 7168], P('ep', 'tp')
The draws below stay inside these ranges and needn't reach their ends.
Inputs may be any that keep to these rules, and one draw needn't show every extreme that they name: `expert_ids`: each row names 8 different experts. In the rows of one device no expert is named more than 12 times, and in every draw some expert is named exactly 12 times there.
All inputs are finite; a program needn't handle non-finite values.
Results may differ from the reference program's by a relative error of at most 0.015.
Values may be sent and summed in bfloat16 or wider, within the bound.
No kernel may reach another device: no remote copies, remote signals or barrier semaphores. Data moves between devices by JAX's collectives and lax.ppermute only.
A program may use at most 128 MiB of HBM per device.

```python
import math
import jax
import jax.numpy as jnp
import numpy as np
from jax import lax

D = 7168
EXP_HID = 1024
EXPERTS = 64
TOP = 8
ROWS_DEV = 64
CAP = 12
ROWS = 4096
N_TP = 4


def shard_levels(own_key, shape, cuts, smallest, top_value):
    level, own = 1.0, jax.random.fold_in(own_key, 6)
    for axis_at, blocks in cuts:
        steps = jnp.exp(jax.random.uniform(jax.random.fold_in(own, axis_at), (blocks,), jnp.float32, smallest / len(cuts), top_value / len(cuts)))
        level = level * jnp.repeat(steps, shape[axis_at] // blocks).reshape([-1 if axis == axis_at else 1 for axis in range(len(shape))])
    return level


def deal_out(rng, own, number, rows, number_of, top, limit, lean):
    order = jax.random.permutation(rng, number_of)
    packed, common = load_shares(number_of, rows * top, limit, lean, True), load_shares(number_of, rows * top, limit, lean, False)
    places = jnp.arange(number_of)

    def named(sizes, rotation):
        used = int((sizes > 0).sum())
        fixed = max(1, used // 4)
        moved = fixed + (places - fixed + rotation * (used - fixed)) % max(1, number_of - fixed)
        return jnp.zeros((number_of,), jnp.int32).at[order[jnp.where(places < fixed, places, moved)]].set(jnp.asarray(sizes, jnp.int32))

    sizes = jnp.where(number % 4 == 0, named(packed, number // 4), named(common, number - number // 4 - 1))
    mixed = jax.random.permutation(jax.random.fold_in(own, 3), number_of)
    giver, receiver = mixed[0:number_of // 2 * 2:2], mixed[1:number_of // 2 * 2:2]
    margin = jnp.minimum(sizes[giver] - 1, limit - sizes[receiver]) // 2
    margin = jnp.where((giver == order[0]) | (receiver == order[0]) | (sizes[receiver] == 0), 0, jnp.maximum(margin, 0))
    moved = jax.random.randint(jax.random.fold_in(own, 4), (number_of // 2,), 0, 1 << 20) % (margin + 1)
    sizes = sizes.at[giver].add(-moved).at[receiver].add(moved)
    labels = jnp.searchsorted(jnp.cumsum(sizes), jnp.arange(rows * top), side="right").astype(jnp.int32)
    listing = labels.reshape(top, rows).T
    listing = listing[jax.random.permutation(jax.random.fold_in(own, 1), rows)]
    rotation = jax.random.randint(jax.random.fold_in(own, 2), (rows, 1), 0, top)
    return jnp.take_along_axis(listing, (jnp.arange(top)[None, :] + rotation) % top, axis=1)


def load_shares(count, total, most, skew, full):
    weights = [(1 << 20) // math.isqrt(grade ** skew) + 1 for grade in range(1, count + 1)]
    largest = most if full else min(most, max(-(-total // count), total * weights[0] // sum(weights)))
    least = 1 if total - largest >= count - 1 else 0
    holding, spare = [largest] + [least] * (count - 1), total - largest - least * (count - 1)
    while spare > 0:
        movable = [i for i in range(1, count) if holding[i] < largest] or [i for i in range(1, count) if holding[i] < most]
        whole, remaining = sum([weights[i] for i in movable]), spare
        for i in movable:
            extra = min(most - holding[i], max(1, remaining * weights[i] // whole), spare)
            holding[i] = holding[i] + extra
            spare = spare - extra
    return np.array(holding)


def gaussian(rng, extent, scale, limit, shards=(), held_as=jnp.bfloat16):
    entries = scale * jax.random.normal(rng, extent, jnp.float32)
    if shards:
        entries = entries * shard_levels(rng, extent, shards, -0.22, 0.18)
    return jnp.clip(entries, -limit, limit).astype(held_as)


def setup_inputs(seed: int = 0) -> dict:
    keys = jax.random.split(jax.random.key(seed), 7)
    hidden_rows = gaussian(keys[0], (ROWS, D), 1.0, 6.0, ((0, 64), (1, 4)))
    expert_ids_keys = jax.random.split(jax.random.fold_in(keys[1], 1), ROWS // ROWS_DEV)
    expert_ids_turns = jax.random.permutation(jax.random.fold_in(keys[1], 3), ROWS // ROWS_DEV)
    expert_ids = jax.vmap(lambda own, number: deal_out(jax.random.fold_in(keys[1], 2), own, number, ROWS_DEV, EXPERTS, TOP, CAP, 2))(expert_ids_keys, expert_ids_turns).reshape((ROWS, TOP))
    affinity = jnp.clip(0.05 + 0.95 * jax.random.uniform(keys[2], (ROWS, TOP), jnp.float32) ** shard_levels(keys[2], (ROWS, TOP), ((0, 64),), -0.2, 0.2), 0.05, 1.0)
    w_gate = gaussian(keys[3], (EXPERTS, D, EXP_HID), D ** -0.5, 0.0625, ((0, 64), (2, 4)))
    w_up = gaussian(keys[4], (EXPERTS, D, EXP_HID), D ** -0.5, 0.0625, ((0, 64), (2, 4)))
    w_down = gaussian(keys[5], (EXPERTS, EXP_HID, D), EXP_HID ** -0.5, 0.1875, ((0, 64), (1, 4)))
    return {"hidden_rows": hidden_rows, "expert_ids": expert_ids, "affinity": affinity, "w_gate": w_gate, "w_up": w_up, "w_down": w_down}


route_scale = 2.5


def reference(hidden_rows, expert_ids, affinity, w_gate, w_up, w_down):
    row_total = hidden_rows.shape[0]
    experts = w_gate.shape[0]
    blocks = row_total // ROWS_DEV
    group_size = w_gate.shape[2] // N_TP
    block_ids = expert_ids.reshape(blocks, ROWS_DEV * TOP)
    onehot = (block_ids[:, :, None] == jnp.arange(experts, dtype=jnp.int32)[None, None, :]).astype(jnp.int32)
    earlier = jnp.cumsum(onehot, axis=1) - onehot
    slot_index = jnp.sum(earlier * onehot, axis=2).astype(jnp.int32)
    route_weight = route_scale * affinity / jnp.sum(affinity, axis=1, keepdims=True)
    flat_expert = block_ids.reshape(-1).astype(jnp.int32)
    flat_block = jnp.repeat(jnp.arange(blocks, dtype=jnp.int32), ROWS_DEV * TOP)
    flat_slot = slot_index.reshape(-1)
    flat_row = jnp.repeat(jnp.arange(row_total, dtype=jnp.int32), TOP)
    slot_rows = jnp.full((experts, blocks, CAP), row_total, jnp.int32)
    slot_rows = slot_rows.at[flat_expert, flat_block, flat_slot].set(flat_row)
    slot_weight = jnp.zeros((experts, blocks, CAP), jnp.float32)
    slot_weight = slot_weight.at[flat_expert, flat_block, flat_slot].set(route_weight.reshape(-1))
    padded_rows = jnp.concatenate([hidden_rows, jnp.zeros((1, hidden_rows.shape[1]), jnp.bfloat16)], axis=0)

    def per_expert(accumulated, inputs):
        rows_here, weight_here, gate_w, up_w, down_w = inputs
        row_index = rows_here.reshape(-1)
        expert_input = padded_rows[row_index]
        gate_proj = jnp.dot(expert_input, gate_w, preferred_element_type=jnp.float32)
        up_proj = jnp.dot(expert_input, up_w, preferred_element_type=jnp.float32)
        activated = (jax.nn.silu(gate_proj) * up_proj).astype(jnp.bfloat16)
        summed = jnp.zeros((expert_input.shape[0], down_w.shape[1]), jnp.float32)
        for group in range(N_TP):
            lower = group * group_size
            partial_down = jnp.dot(activated[:, lower:lower + group_size], down_w[lower:lower + group_size, :], preferred_element_type=jnp.float32).astype(jnp.bfloat16)
            partial_down = lax.optimization_barrier(partial_down)
            summed = summed + partial_down.astype(jnp.float32)
        expert_output = lax.optimization_barrier(summed.astype(jnp.bfloat16)).astype(jnp.float32)
        accumulated = accumulated.at[row_index].add(weight_here.reshape(-1)[:, None] * expert_output)
        return accumulated, None

    start = jnp.zeros((row_total + 1, hidden_rows.shape[1]), jnp.float32)
    accumulated, unused = lax.scan(per_expert, start, (slot_rows, slot_weight, w_gate, w_up, w_down))
    return accumulated[:row_total].astype(jnp.bfloat16)
```

```python
import functools

import jax
import jax.numpy as jnp
from jax import lax
from jax.experimental import pallas as pl
from jax.experimental.pallas import tpu as pltpu
from jax.sharding import PartitionSpec as P

CAP = 12
CHUNKS = ((0, 8), (8, 4))
VMEM_LIMIT = 48 * 1024 * 1024


route_scale = 2.5


def hidden_kernel(x_ref, gate_ref, up_ref, out_ref, gate_sum, up_sum):
    step = pl.program_id(0)
    x = x_ref[0]
    gate_part = jnp.dot(x, gate_ref[0], preferred_element_type=jnp.float32)
    up_part = jnp.dot(x, up_ref[0], preferred_element_type=jnp.float32)

    @pl.when(step == 0)
    def _():
        gate_sum[...] = gate_part
        up_sum[...] = up_part

    @pl.when(step > 0)
    def _():
        gate_sum[...] += gate_part
        up_sum[...] += up_part

    @pl.when(step == pl.num_programs(0) - 1)
    def _():
        gate = gate_sum[...]
        out_ref[...] = (gate / (1.0 + jnp.exp(-gate)) * up_sum[...]).astype(out_ref.dtype)


def hidden_units(x, w_gate, w_up):
    parts, rows, width = x.shape
    hidden = w_gate.shape[1]
    w_gate = w_gate.reshape(parts, width, hidden)
    w_up = w_up.reshape(parts, width, hidden)
    return pl.pallas_call(
        hidden_kernel,
        grid=(parts,),
        in_specs=[
            pl.BlockSpec((1, rows, width), lambda i: (i, 0, 0)),
            pl.BlockSpec((1, width, hidden), lambda i: (i, 0, 0)),
            pl.BlockSpec((1, width, hidden), lambda i: (i, 0, 0)),
        ],
        out_specs=pl.BlockSpec((rows, hidden), lambda i: (0, 0)),
        out_shape=jax.ShapeDtypeStruct((rows, hidden), jnp.bfloat16),
        scratch_shapes=[pltpu.VMEM((rows, hidden), jnp.float32), pltpu.VMEM((rows, hidden), jnp.float32)],
        compiler_params=pltpu.CompilerParams(vmem_limit_bytes=VMEM_LIMIT),
        cost_estimate=pl.CostEstimate(
            flops=4 * rows * parts * width * hidden,
            bytes_accessed=2 * parts * width * (rows + 2 * hidden) + 2 * rows * hidden,
            transcendentals=rows * hidden,
        ),
        name="hidden_units",
    )(x, w_gate, w_up)


def down_kernel(a_ref, w_ref, out_ref):
    total = jnp.dot(a_ref[0], w_ref[0], preferred_element_type=jnp.float32)
    for part in range(1, a_ref.shape[0]):
        total += jnp.dot(a_ref[part], w_ref[part], preferred_element_type=jnp.float32)
    out_ref[...] = total.astype(out_ref.dtype)


def down(act, w_down):
    parts, rows, hidden = act.shape
    width = w_down.shape[2]
    tile = 256
    return pl.pallas_call(
        down_kernel,
        grid=(width // tile,),
        in_specs=[
            pl.BlockSpec((parts, rows, hidden), lambda i: (0, 0, 0)),
            pl.BlockSpec((parts, hidden, tile), lambda i: (0, 0, i)),
        ],
        out_specs=pl.BlockSpec((rows, tile), lambda i: (0, i)),
        out_shape=jax.ShapeDtypeStruct((rows, width), jnp.bfloat16),
        compiler_params=pltpu.CompilerParams(vmem_limit_bytes=VMEM_LIMIT),
        cost_estimate=pl.CostEstimate(
            flops=2 * rows * parts * hidden * width,
            bytes_accessed=2 * (parts * hidden * (rows + width) + rows * width),
            transcendentals=0,
        ),
        name="down",
    )(act, w_down)


def on_device(hidden_rows, expert_ids, affinity, w_gate, w_up, w_down):
    experts = lax.axis_size("ep")
    tp_count = lax.axis_size("tp")
    row_count, width = hidden_rows.shape
    w_gate, w_up, w_down = w_gate[0], w_up[0], w_down[0]

    down_rows = lax.all_to_all(
        w_down.reshape(w_down.shape[0], tp_count, width), "tp", split_axis=1, concat_axis=1, tiled=True
    )
    down_rows = down_rows.transpose(1, 0, 2)

    route_weight = route_scale * affinity / jnp.sum(affinity, axis=1, keepdims=True)
    named = expert_ids[:, :, None] == jnp.arange(experts, dtype=jnp.int32)
    chosen = jnp.any(named, axis=1)
    weight = jnp.sum(jnp.where(named, route_weight[:, :, None], 0.0), axis=1)
    earlier = jnp.tril(jnp.ones((row_count, row_count), jnp.bfloat16), -1)
    slot = jnp.dot(earlier, chosen.astype(jnp.bfloat16), preferred_element_type=jnp.float32).astype(jnp.int32)
    slot = jnp.where(chosen, slot, CAP)

    places, arrived = [], []
    for first, count in CHUNKS:
        here = slot[:, :, None] == first + jnp.arange(count, dtype=jnp.int32)
        places.append(here.reshape(row_count, experts * count))
        outgoing = jnp.dot(
            places[-1].astype(jnp.bfloat16).T, hidden_rows, preferred_element_type=jnp.float32
        ).astype(jnp.bfloat16)
        outgoing = outgoing.reshape(experts, count, width)
        arrived.append(lax.all_to_all(outgoing, "ep", split_axis=0, concat_axis=0, tiled=True))

    mixed = jnp.zeros((row_count, width), jnp.float32)
    for (first, count), place, rows in zip(CHUNKS, places, arrived):
        x = lax.all_gather(rows.reshape(experts * count, width), "tp")
        activated = hidden_units(x, w_gate, w_up)
        activated = lax.all_gather(activated, "tp")
        outputs = down(activated, down_rows).reshape(experts, count, width)
        returned = lax.all_to_all(outputs, "ep", split_axis=0, concat_axis=0, tiled=True)
        returned = returned.reshape(experts * count, width)
        mix = jnp.where(place, jnp.repeat(weight, count, axis=1), 0.0)
        high = mix.astype(jnp.bfloat16)
        low = (mix - high.astype(jnp.float32)).astype(jnp.bfloat16)
        mixed = mixed + jnp.dot(high, returned, preferred_element_type=jnp.float32)
        mixed = mixed + jnp.dot(low, returned, preferred_element_type=jnp.float32)
    return mixed.astype(jnp.bfloat16)


def solution(mesh):
    in_specs = (
        P("ep", "tp"),
        P("ep", None),
        P("ep", None),
        P("ep", None, "tp"),
        P("ep", None, "tp"),
        P("ep", "tp", None),
    )
    out_specs = P("ep", "tp")
    return jax.shard_map(
        on_device, mesh=mesh, in_specs=in_specs, out_specs=out_specs, check_vma=False
    )
```

```python
import functools

import jax
import jax.numpy as jnp
from jax import lax
from jax.experimental import pallas as pl
from jax.experimental.pallas import tpu as pltpu
from jax.sharding import PartitionSpec as P

CAP = 12
CHUNKS = ((0, 4), (4, 4), (8, 4))
MIB = 1024 * 1024
CORNER = pl.BlockSpec((16, 128), lambda *index: (0, 0))


route_scale = 2.5


def near_kernel(me_ref, own_a, own_b, left_a, left_b, right_a, right_b, gate_own, gate_left, gate_right,
                up_own, up_left, up_right, out_ref):
    half = own_a.shape[0]
    hidden = gate_own.shape[2]
    for row, blocks in ((0, (own_a, left_a, right_a)), (half, (own_b, left_b, right_b))):
        for column, weights in ((0, (gate_own, gate_left, gate_right)), (hidden, (up_own, up_left, up_right))):
            total = jnp.dot(blocks[0][...], weights[0][0], preferred_element_type=jnp.float32)
            for block, weight in zip(blocks[1:], weights[1:]):
                total += jnp.dot(block[...], weight[0], preferred_element_type=jnp.float32)
            out_ref[row:row + half, column:column + hidden] = total


def far_kernel(me_ref, near_ref, far_a, far_b, gate_far, up_far, *rest):
    out_ref = rest[-1]
    half = far_a.shape[0]
    hidden = gate_far.shape[2]
    for row, block in ((0, far_a), (half, far_b)):
        gate = near_ref[row:row + half, :hidden] + jnp.dot(
            block[...], gate_far[0], preferred_element_type=jnp.float32
        )
        up = near_ref[row:row + half, hidden:] + jnp.dot(block[...], up_far[0], preferred_element_type=jnp.float32)
        out_ref[row:row + half, :] = (gate / (1.0 + jnp.exp(-gate)) * up).astype(out_ref.dtype)


def hidden_near(me, blocks, w_gate, w_up):
    parts, width, hidden = w_gate.shape
    half = blocks[0].shape[0]
    row_spec = pl.BlockSpec((half, width), lambda i, me: (0, 0))
    weight_specs = [
        pl.BlockSpec((1, width, hidden), lambda i, me, step=step: (lax.rem(me[0] + step, parts), 0, 0))
        for step in (0, parts - 1, 1)
    ]
    return pl.pallas_call(
        near_kernel,
        grid_spec=pltpu.PrefetchScalarGridSpec(
            num_scalar_prefetch=1,
            grid=(1,),
            in_specs=[row_spec] * 6 + weight_specs * 2,
            out_specs=pl.BlockSpec((2 * half, 2 * hidden), lambda i, me: (0, 0)),
        ),
        out_shape=jax.ShapeDtypeStruct((2 * half, 2 * hidden), jnp.float32),
        compiler_params=pltpu.CompilerParams(vmem_limit_bytes=24 * MIB),
        cost_estimate=pl.CostEstimate(
            flops=24 * half * width * hidden,
            bytes_accessed=12 * width * (half + hidden) + 16 * half * hidden,
            transcendentals=0,
        ),
        name="hidden_near",
    )(me, *blocks, w_gate, w_gate, w_gate, w_up, w_up, w_up)


def hidden_far(me, near, far_a, far_b, w_gate, w_up, after):
    parts, width, hidden = w_gate.shape
    half = far_a.shape[0]
    row_spec = pl.BlockSpec((half, width), lambda i, me: (0, 0))
    weight_spec = pl.BlockSpec((1, width, hidden), lambda i, me: (lax.rem(me[0] + 2, parts), 0, 0))
    return pl.pallas_call(
        far_kernel,
        grid_spec=pltpu.PrefetchScalarGridSpec(
            num_scalar_prefetch=1,
            grid=(1,),
            in_specs=[pl.BlockSpec((2 * half, 2 * hidden), lambda i, me: (0, 0))]
            + [row_spec] * 2 + [weight_spec] * 2 + [CORNER] * len(after),
            out_specs=pl.BlockSpec((2 * half, hidden), lambda i, me: (0, 0)),
        ),
        out_shape=jax.ShapeDtypeStruct((2 * half, hidden), jnp.bfloat16),
        compiler_params=pltpu.CompilerParams(vmem_limit_bytes=12 * MIB),
        cost_estimate=pl.CostEstimate(
            flops=8 * half * width * hidden,
            bytes_accessed=4 * width * (half + hidden) + 20 * half * hidden,
            transcendentals=2 * half * hidden,
        ),
        name="hidden_far",
    )(me, near, far_a, far_b, w_gate, w_up, *after)


def down_kernel(count, me_ref, *refs):
    acts, weights, out_ref = refs[:count], refs[count:2 * count], refs[-1]
    total = jnp.dot(acts[0][...], weights[0][...], preferred_element_type=jnp.float32)
    for act, weight in zip(acts[1:], weights[1:]):
        total += jnp.dot(act[...], weight[...], preferred_element_type=jnp.float32)
    out_ref[...] = total.astype(out_ref.dtype)


def down(me, acts, w_down, pieces, after):
    rows, hidden = acts[0].shape
    width = pieces[0].shape[1]
    parts = len(acts)
    tile = 896
    tiles = width // tile
    return pl.pallas_call(
        functools.partial(down_kernel, parts),
        grid_spec=pltpu.PrefetchScalarGridSpec(
            num_scalar_prefetch=1,
            grid=(tiles,),
            in_specs=[pl.BlockSpec((rows, hidden), lambda i, me: (0, 0))] * parts
            + [pl.BlockSpec((hidden, tile), lambda i, me: (0, me[0] * tiles + i))]
            + [pl.BlockSpec((hidden, tile), lambda i, me: (0, i))] * (parts - 1)
            + [CORNER] * len(after),
            out_specs=pl.BlockSpec((rows, tile), lambda i, me: (0, i)),
        ),
        out_shape=jax.ShapeDtypeStruct((rows, width), jnp.bfloat16),
        compiler_params=pltpu.CompilerParams(vmem_limit_bytes=12 * MIB),
        cost_estimate=pl.CostEstimate(
            flops=2 * rows * parts * hidden * width,
            bytes_accessed=2 * (parts * hidden * (rows + width) + rows * width),
            transcendentals=0,
        ),
        name="down",
    )(me, *acts, w_down, *pieces, *after)


def place_kernel(spot_ref, rows_ref, *rest):
    out_ref = rest[-1]
    out_ref[...] = lax.dot_general(
        spot_ref[...], rows_ref[...], (((0,), (0,)), ((), ())), preferred_element_type=jnp.float32
    ).astype(out_ref.dtype)


def place_rows(spot, rows, after):
    slots, width = spot.shape[1], rows.shape[1]
    return pl.pallas_call(
        place_kernel,
        grid=(1,),
        in_specs=[
            pl.BlockSpec((rows.shape[0], slots), lambda i: (0, 0)),
            pl.BlockSpec((rows.shape[0], width), lambda i: (0, 0)),
        ]
        + [CORNER] * len(after),
        out_specs=pl.BlockSpec((slots, width), lambda i: (0, 0)),
        out_shape=jax.ShapeDtypeStruct((slots, width), jnp.bfloat16),
        compiler_params=pltpu.CompilerParams(vmem_limit_bytes=8 * MIB),
        cost_estimate=pl.CostEstimate(
            flops=2 * slots * rows.shape[0] * width,
            bytes_accessed=2 * (slots + rows.shape[0]) * width,
            transcendentals=0,
        ),
        name="place_rows",
    )(spot, rows, *after)


def on_device(hidden_rows, expert_ids, affinity, w_gate, w_up, w_down):
    experts = lax.axis_size("ep")
    parts = lax.axis_size("tp")
    row_count, width = hidden_rows.shape
    place = lax.axis_index("tp")
    me = place.reshape(1).astype(jnp.int32)
    w_gate = w_gate[0].reshape(parts, width, w_gate.shape[2])
    w_up = w_up[0].reshape(parts, width, w_up.shape[2])
    w_down = w_down[0]

    def send(array, step):
        return lax.ppermute(array, "tp", [(i, (i + step) % parts) for i in range(parts)])

    pieces = [
        send(lax.dynamic_slice_in_dim(w_down, (place + step) % parts * width, width, axis=1), step)
        for step in (1, parts - 1, 2)
    ]

    route_weight = route_scale * affinity / jnp.sum(affinity, axis=1, keepdims=True)
    named = expert_ids[:, :, None] == jnp.arange(experts, dtype=jnp.int32)
    chosen = jnp.any(named, axis=1)
    weight = jnp.sum(jnp.where(named, route_weight[:, :, None], 0.0), axis=1)
    earlier = jnp.tril(jnp.ones((row_count, row_count), jnp.bfloat16), -1)
    slot = jnp.dot(earlier, chosen.astype(jnp.bfloat16), preferred_element_type=jnp.float32).astype(jnp.int32)
    slot = jnp.where(chosen, slot, CAP)

    places, near_blocks, far_blocks = [], [], []
    for number, (first, count) in enumerate(CHUNKS):
        here = slot[:, :, None] == first + jnp.arange(count, dtype=jnp.int32)
        places.append(here.reshape(row_count, experts * count))
        after = () if number == 0 else pieces if number == 1 else far_blocks[number - 2]
        outgoing = place_rows(places[-1].astype(jnp.bfloat16), hidden_rows, after)
        outgoing = outgoing.reshape(experts, count, width)
        rows = lax.all_to_all(outgoing, "ep", split_axis=0, concat_axis=0, tiled=True)
        half = experts // 2
        own_a = rows[:half].reshape(half * count, width)
        own_b = rows[half:].reshape(half * count, width)
        left_a, right_b = send(own_a, 1), send(own_b, -1)
        left_b, right_a = send(own_b, 1), send(own_a, -1)
        near_blocks.append((own_a, own_b, left_a, left_b, right_a, right_b))
        far_blocks.append((send(left_a, 1), send(right_b, -1)))

    mixed = jnp.zeros((row_count, width), jnp.float32)
    for number, ((first, count), spot) in enumerate(zip(CHUNKS, places)):
        near = hidden_near(me, near_blocks[number], w_gate, w_up)
        after = near_blocks[number + 1][2:] if number + 1 < len(CHUNKS) else ()
        activated = hidden_far(me, near, *far_blocks[number], w_gate, w_up, after)
        acts = [activated] + [send(activated, step) for step in (1, parts - 1, 2)]
        after = far_blocks[number + 1] if number + 1 < len(CHUNKS) else ()
        outputs = down(me, acts, w_down, pieces, after).reshape(experts, count, width)
        returned = lax.all_to_all(outputs, "ep", split_axis=0, concat_axis=0, tiled=True)
        returned = returned.reshape(experts * count, width)
        mix = jnp.where(spot, jnp.repeat(weight, count, axis=1), 0.0)
        high = mix.astype(jnp.bfloat16)
        low = (mix - high.astype(jnp.float32)).astype(jnp.bfloat16)
        mixed = mixed + jnp.dot(high, returned, preferred_element_type=jnp.float32)
        mixed = mixed + jnp.dot(low, returned, preferred_element_type=jnp.float32)
    return mixed.astype(jnp.bfloat16)


def solution(mesh):
    in_specs = (
        P("ep", "tp"),
        P("ep", None),
        P("ep", None),
        P("ep", None, "tp"),
        P("ep", None, "tp"),
        P("ep", "tp", None),
    )
    out_specs = P("ep", "tp")
    return jax.shard_map(
        on_device, mesh=mesh, in_specs=in_specs, out_specs=out_specs, check_vma=False
    )
```

```python
import functools

import jax
import jax.numpy as jnp
from jax import lax
from jax.experimental import pallas as pl
from jax.experimental.pallas import tpu as pltpu
from jax.sharding import PartitionSpec as P

CAP = 12
CHUNKS = ((0, 4, False), (4, 4, True), (8, 4, False))
TOLD = (100, 100, 1)
MIB = 1024 * 1024
CORNER = pl.BlockSpec((16, 128), lambda *index: (0, 0))
CORNER_SLOTS = pl.BlockSpec((8, 4, 128), lambda *index: (0, 0, 0))


route_scale = 2.5


def store_slots(out_ref, total):
    count = out_ref.shape[1]
    for expert in range(out_ref.shape[0]):
        out_ref[expert] = total[expert * count:(expert + 1) * count].astype(out_ref.dtype)


def silu_times(gate, up):
    return gate / (1.0 + jnp.exp(-gate)) * up


def gathered_kernel(x_ref, gate_ref, up_ref, *rest):
    out_ref, gate_sum, up_sum = rest[-3:]
    step = pl.program_id(0)
    x = x_ref[0]
    gate_part = jnp.dot(x, gate_ref[0], preferred_element_type=jnp.float32)
    up_part = jnp.dot(x, up_ref[0], preferred_element_type=jnp.float32)

    @pl.when(step == 0)
    def _():
        gate_sum[...] = gate_part
        up_sum[...] = up_part

    @pl.when(step > 0)
    def _():
        gate_sum[...] += gate_part
        up_sum[...] += up_part

    @pl.when(step == pl.num_programs(0) - 1)
    def _():
        out_ref[...] = silu_times(gate_sum[...], up_sum[...]).astype(out_ref.dtype)


def hidden_gathered(x, w_gate, w_up, told):
    parts, rows, width = x.shape
    hidden = w_gate.shape[2]
    return pl.pallas_call(
        gathered_kernel,
        grid=(parts,),
        in_specs=[
            pl.BlockSpec((1, rows, width), lambda i: (i, 0, 0)),
            pl.BlockSpec((1, width, hidden), lambda i: (i, 0, 0)),
            pl.BlockSpec((1, width, hidden), lambda i: (i, 0, 0)),
        ],
        out_specs=pl.BlockSpec((rows, hidden), lambda i: (0, 0)),
        out_shape=jax.ShapeDtypeStruct((rows, hidden), jnp.bfloat16),
        scratch_shapes=[pltpu.VMEM((rows, hidden), jnp.float32), pltpu.VMEM((rows, hidden), jnp.float32)],
        compiler_params=pltpu.CompilerParams(vmem_limit_bytes=16 * MIB),
        cost_estimate=pl.CostEstimate(
            flops=4 * rows * parts * width * hidden * told,
            bytes_accessed=2 * parts * width * (rows + 2 * hidden) + 2 * rows * hidden,
            transcendentals=rows * hidden,
        ),
        name="hidden_gathered",
    )(x, w_gate, w_up)


def near_kernel(me_ref, own, left, right, gate_own, gate_left, gate_right, up_own, up_left, up_right, *rest):
    out_ref = rest[-1]
    hidden = gate_own.shape[2]
    for column, weights in ((0, (gate_own, gate_left, gate_right)), (hidden, (up_own, up_left, up_right))):
        total = jnp.dot(own[...], weights[0][0], preferred_element_type=jnp.float32)
        total += jnp.dot(left[...], weights[1][0], preferred_element_type=jnp.float32)
        total += jnp.dot(right[...], weights[2][0], preferred_element_type=jnp.float32)
        out_ref[:, column:column + hidden] = total


def hidden_near(me, blocks, w_gate, w_up, after, told):
    parts, width, hidden = w_gate.shape
    rows = blocks[0].shape[0]
    row_spec = pl.BlockSpec((rows, width), lambda i, me: (0, 0))
    weight_specs = [
        pl.BlockSpec((1, width, hidden), lambda i, me, step=step: (lax.rem(me[0] + step, parts), 0, 0))
        for step in (0, parts - 1, 1)
    ]
    return pl.pallas_call(
        near_kernel,
        grid_spec=pltpu.PrefetchScalarGridSpec(
            num_scalar_prefetch=1,
            grid=(1,),
            in_specs=[row_spec] * 3 + weight_specs * 2 + [CORNER] * len(after),
            out_specs=pl.BlockSpec((rows, 2 * hidden), lambda i, me: (0, 0)),
        ),
        out_shape=jax.ShapeDtypeStruct((rows, 2 * hidden), jnp.float32),
        compiler_params=pltpu.CompilerParams(vmem_limit_bytes=24 * MIB),
        cost_estimate=pl.CostEstimate(
            flops=12 * rows * width * hidden * told,
            bytes_accessed=6 * width * (rows + 2 * hidden) + 8 * rows * hidden,
            transcendentals=0,
        ),
        name="hidden_near",
    )(me, *blocks, w_gate, w_gate, w_gate, w_up, w_up, w_up, *after)


def far_kernel(me_ref, near_ref, far, gate_far, up_far, out_ref):
    hidden = gate_far.shape[2]
    gate = near_ref[:, :hidden] + jnp.dot(far[...], gate_far[0], preferred_element_type=jnp.float32)
    up = near_ref[:, hidden:] + jnp.dot(far[...], up_far[0], preferred_element_type=jnp.float32)
    out_ref[...] = silu_times(gate, up).astype(out_ref.dtype)


def hidden_far(me, near, far, w_gate, w_up):
    parts, width, hidden = w_gate.shape
    rows = far.shape[0]
    weight_spec = pl.BlockSpec((1, width, hidden), lambda i, me: (lax.rem(me[0] + 2, parts), 0, 0))
    return pl.pallas_call(
        far_kernel,
        grid_spec=pltpu.PrefetchScalarGridSpec(
            num_scalar_prefetch=1,
            grid=(1,),
            in_specs=[
                pl.BlockSpec((rows, 2 * hidden), lambda i, me: (0, 0)),
                pl.BlockSpec((rows, width), lambda i, me: (0, 0)),
                weight_spec,
                weight_spec,
            ],
            out_specs=pl.BlockSpec((rows, hidden), lambda i, me: (0, 0)),
        ),
        out_shape=jax.ShapeDtypeStruct((rows, hidden), jnp.bfloat16),
        compiler_params=pltpu.CompilerParams(vmem_limit_bytes=12 * MIB),
        cost_estimate=pl.CostEstimate(
            flops=4 * rows * width * hidden,
            bytes_accessed=2 * width * (rows + 2 * hidden) + 10 * rows * hidden,
            transcendentals=rows * hidden,
        ),
        name="hidden_far",
    )(me, near, far, w_gate, w_up)


def down_kernel(parts, me_ref, *refs):
    acts, weights, out_ref = refs[:parts], refs[parts:2 * parts], refs[-1]
    total = jnp.dot(acts[0][...], weights[0][...], preferred_element_type=jnp.float32)
    for act, weight in zip(acts[1:], weights[1:]):
        total += jnp.dot(act[...], weight[...], preferred_element_type=jnp.float32)
    store_slots(out_ref, total)


def down(me, acts, w_down, pieces, experts):
    rows, hidden = acts[0].shape
    width = pieces[0].shape[1]
    parts = len(acts)
    tile = 896
    tiles = width // tile
    return pl.pallas_call(
        functools.partial(down_kernel, parts),
        grid_spec=pltpu.PrefetchScalarGridSpec(
            num_scalar_prefetch=1,
            grid=(tiles,),
            in_specs=[pl.BlockSpec((rows, hidden), lambda i, me: (0, 0))] * parts
            + [pl.BlockSpec((hidden, tile), lambda i, me: (0, me[0] * tiles + i))]
            + [pl.BlockSpec((hidden, tile), lambda i, me: (0, i))] * (parts - 1),
            out_specs=pl.BlockSpec((experts, rows // experts, tile), lambda i, me: (0, 0, i)),
        ),
        out_shape=jax.ShapeDtypeStruct((experts, rows // experts, width), jnp.bfloat16),
        compiler_params=pltpu.CompilerParams(vmem_limit_bytes=16 * MIB),
        cost_estimate=pl.CostEstimate(
            flops=2 * rows * parts * hidden * width,
            bytes_accessed=2 * (parts * hidden * (rows + width) + rows * width),
            transcendentals=0,
        ),
        name="down",
    )(me, *acts, w_down, *pieces)


def place_kernel(spot_ref, rows_ref, *rest):
    total = lax.dot_general(
        spot_ref[...], rows_ref[...], (((0,), (0,)), ((), ())), preferred_element_type=jnp.float32
    )
    store_slots(rest[-1], total)


def place_rows(spot, rows, experts, after, weight):
    slots, width = spot.shape[1], rows.shape[1]
    tile = 896
    return pl.pallas_call(
        place_kernel,
        grid=(width // tile,),
        in_specs=[
            pl.BlockSpec((rows.shape[0], slots), lambda i: (0, 0)),
            pl.BlockSpec((rows.shape[0], tile), lambda i: (0, i)),
        ]
        + [CORNER if array.ndim == 2 else CORNER_SLOTS for array in after],
        out_specs=pl.BlockSpec((experts, slots // experts, tile), lambda i: (0, 0, i)),
        out_shape=jax.ShapeDtypeStruct((experts, slots // experts, width), jnp.bfloat16),
        compiler_params=pltpu.CompilerParams(vmem_limit_bytes=12 * MIB),
        cost_estimate=pl.CostEstimate(
            flops=2 * slots * rows.shape[0] * width * weight,
            bytes_accessed=2 * (slots + rows.shape[0]) * width,
            transcendentals=0,
        ),
        name="place_rows",
    )(spot, rows, *after)


def on_device(hidden_rows, expert_ids, affinity, w_gate, w_up, w_down):
    experts = lax.axis_size("ep")
    parts = lax.axis_size("tp")
    row_count, width = hidden_rows.shape
    place = lax.axis_index("tp")
    me = place.reshape(1).astype(jnp.int32)
    w_gate = w_gate[0].reshape(parts, width, w_gate.shape[2])
    w_up = w_up[0].reshape(parts, width, w_up.shape[2])
    w_down = w_down[0]

    def send(array, step):
        return lax.ppermute(array, "tp", [(i, (i + step) % parts) for i in range(parts)])

    def send_all(array):
        return [send(array, step) for step in (1, parts - 1, 2)]

    slices = [
        lax.dynamic_slice_in_dim(w_down, (place + step) % parts * width, width, axis=1) for step in (1, parts - 1, 2)
    ]
    pieces = [send(part, step) for part, step in zip(slices, (1, parts - 1, 2))]

    route_weight = route_scale * affinity / jnp.sum(affinity, axis=1, keepdims=True)
    named = expert_ids[:, :, None] == jnp.arange(experts, dtype=jnp.int32)
    chosen = jnp.any(named, axis=1)
    weight = jnp.sum(jnp.where(named, route_weight[:, :, None], 0.0), axis=1)
    earlier = jnp.tril(jnp.ones((row_count, row_count), jnp.bfloat16), -1)
    slot = jnp.dot(earlier, chosen.astype(jnp.bfloat16), preferred_element_type=jnp.float32).astype(jnp.int32)
    slot = jnp.where(chosen, slot, CAP)

    places, gathered = [], []
    for number, (first, count, by_permutes) in enumerate(CHUNKS):
        here = slot[:, :, None] == first + jnp.arange(count, dtype=jnp.int32)
        places.append(here.reshape(row_count, experts * count))
        after = slices if number == 0 else [*pieces, before] if number == 1 else [before]
        outgoing = place_rows(places[-1].astype(jnp.bfloat16), hidden_rows, experts, after, (1, 2000, 1)[number])
        rows = lax.all_to_all(outgoing, "ep", split_axis=0, concat_axis=0, tiled=True)
        before = rows
        rows = rows.reshape(experts * count, width)
        gathered.append([rows] + send_all(rows) if by_permutes else lax.all_gather(rows, "tp"))

    mixed = jnp.zeros((row_count, width), jnp.float32)
    for (first, count, by_permutes), spot, x, told in zip(CHUNKS, places, gathered, TOLD):
        if by_permutes:
            near = hidden_near(me, x[:3], w_gate, w_up, [activated, x[3]], told)
            activated = hidden_far(me, near, x[3], w_gate, w_up)
        else:
            activated = hidden_gathered(x, w_gate, w_up, told)
        outputs = down(me, [activated] + send_all(activated), w_down, pieces, experts)
        returned = lax.all_to_all(outputs, "ep", split_axis=0, concat_axis=0, tiled=True)
        returned = returned.reshape(experts * count, width)
        mix = jnp.where(spot, jnp.repeat(weight, count, axis=1), 0.0)
        high = mix.astype(jnp.bfloat16)
        low = (mix - high.astype(jnp.float32)).astype(jnp.bfloat16)
        mixed = mixed + jnp.dot(high, returned, preferred_element_type=jnp.float32)
        mixed = mixed + jnp.dot(low, returned, preferred_element_type=jnp.float32)
    return mixed.astype(jnp.bfloat16)


def solution(mesh):
    in_specs = (
        P("ep", "tp"),
        P("ep", None),
        P("ep", None),
        P("ep", None, "tp"),
        P("ep", None, "tp"),
        P("ep", "tp", None),
    )
    out_specs = P("ep", "tp")
    return jax.shard_map(
        on_device, mesh=mesh, in_specs=in_specs, out_specs=out_specs, check_vma=False
    )
```

```python
import functools

import jax
import jax.numpy as jnp
from jax import lax
from jax.experimental import pallas as pl
from jax.experimental.pallas import tpu as pltpu
from jax.sharding import PartitionSpec as P

CAP = 12
CHUNKS = ((0, 4, False), (4, 4, True), (8, 4, False))
SENDS = (1, 3, 2)
STEPS = (0, 3, 1, 2)
TILES = 2
TOLD = (100, 100, 1)
WAIT_TOLD = 200_000_000_000
MIB = 1024 * 1024
CORNER = pl.BlockSpec((16, 128), lambda *index: (0, 0))
IN_HBM = pl.BlockSpec(memory_space=pltpu.HBM)
CORNER_SLOTS = pl.BlockSpec((8, 4, 128), lambda *index: (0, 0, 0))


route_scale = 2.5


def store_slots(out_ref, total):
    count = out_ref.shape[1]
    for expert in range(out_ref.shape[0]):
        out_ref[expert] = total[expert * count:(expert + 1) * count].astype(out_ref.dtype)


def silu_times(gate, up):
    return gate / (1.0 + jnp.exp(-gate)) * up


def hidden_kernel(gathered, parts, me_ref, *refs):
    arrays = 1 if gathered else parts
    xs, (gate_ref, up_ref) = refs[:arrays], refs[arrays:arrays + 2]
    out_ref, x_buffer, gate_buffer, up_buffer, gate_sum, up_sum, arrivals = refs[-7:]
    copies = []
    for number, step in enumerate(range(parts) if gathered else STEPS):
        part = step if gathered else lax.rem(me_ref[0] + step, parts)
        x_part = xs[0].at[step] if gathered else xs[number]
        pairs = (
            (x_part, x_buffer.at[number]),
            (gate_ref.at[part], gate_buffer.at[number]),
            (up_ref.at[part], up_buffer.at[number]),
        )
        copies.append(
            [pltpu.make_async_copy(a, b, arrivals.at[number, i]) for i, (a, b) in enumerate(pairs)]
        )
        for copy in copies[-1]:
            copy.start()
    for number in range(parts):
        for copy in copies[number]:
            copy.wait()
        x = x_buffer[number]
        gate_part = jnp.dot(x, gate_buffer[number], preferred_element_type=jnp.float32)
        up_part = jnp.dot(x, up_buffer[number], preferred_element_type=jnp.float32)
        if number == 0:
            gate_sum[...] = gate_part
            up_sum[...] = up_part
        elif number < parts - 1:
            gate_sum[...] += gate_part
            up_sum[...] += up_part
        else:
            out_ref[...] = silu_times(gate_sum[...] + gate_part, up_sum[...] + up_part).astype(out_ref.dtype)


def hidden_units(me, xs, w_gate, w_up, after, told):
    gathered = len(xs) == 1
    parts, width, hidden = w_gate.shape
    rows = xs[0].shape[-2]
    return pl.pallas_call(
        functools.partial(hidden_kernel, gathered, parts),
        grid_spec=pltpu.PrefetchScalarGridSpec(
            num_scalar_prefetch=1,
            grid=(1,),
            in_specs=[IN_HBM] * (len(xs) + 2) + [CORNER] * len(after),
            out_specs=pl.BlockSpec((rows, hidden), lambda i, me: (0, 0)),
            scratch_shapes=[
                pltpu.VMEM((parts, rows, width), jnp.bfloat16),
                pltpu.VMEM((parts, width, hidden), jnp.bfloat16),
                pltpu.VMEM((parts, width, hidden), jnp.bfloat16),
                pltpu.VMEM((rows, hidden), jnp.float32),
                pltpu.VMEM((rows, hidden), jnp.float32),
                pltpu.SemaphoreType.DMA((parts, 3)),
            ],
        ),
        out_shape=jax.ShapeDtypeStruct((rows, hidden), jnp.bfloat16),
        compiler_params=pltpu.CompilerParams(vmem_limit_bytes=60 * MIB),
        cost_estimate=pl.CostEstimate(
            flops=4 * rows * parts * width * hidden * told,
            bytes_accessed=2 * parts * width * (rows + 2 * hidden) + 2 * rows * hidden,
            transcendentals=rows * hidden,
        ),
        name="hidden_units",
    )(me, *xs, w_gate, w_up, *after)


def down_kernel(parts, me_ref, *refs):
    acts, own_ref, pieces = refs[:parts], refs[parts], refs[parts + 1:2 * parts]
    out_ref, weights, slots, arrivals, departures = refs[-5:]
    width = slots.shape[2]
    tile = width // TILES
    copies = []
    for number in range(TILES):
        sources = [own_ref.at[:, pl.ds(pl.multiple_of(me_ref[0] * width + number * tile, 128), tile)]]
        sources += [piece.at[:, pl.ds(number * tile, tile)] for piece in pieces]
        copies.append([
            pltpu.make_async_copy(source, weights.at[number, i], arrivals.at[number, i])
            for i, source in enumerate(sources)
        ])
        for copy in copies[-1]:
            copy.start()
    leaving = []
    for number in range(TILES):
        for copy in copies[number]:
            copy.wait()
        total = jnp.dot(acts[0][...], weights[number, 0], preferred_element_type=jnp.float32)
        for i in range(1, parts):
            total += jnp.dot(acts[i][...], weights[number, i], preferred_element_type=jnp.float32)
        store_slots(slots.at[:, :, pl.ds(number * tile, tile)], total)
        where = pl.ds(number * tile, tile)
        leaving.append(
            pltpu.make_async_copy(slots.at[:, :, where], out_ref.at[:, :, where], departures.at[number])
        )
        leaving[-1].start()
    for copy in leaving:
        copy.wait()


def down(me, acts, w_down, pieces, experts):
    rows, hidden = acts[0].shape
    width = pieces[0].shape[1]
    parts = len(acts)
    shape = (experts, rows // experts, width)
    return pl.pallas_call(
        functools.partial(down_kernel, parts),
        grid_spec=pltpu.PrefetchScalarGridSpec(
            num_scalar_prefetch=1,
            grid=(1,),
            in_specs=[pl.BlockSpec((rows, hidden), lambda i, me: (0, 0))] * parts + [IN_HBM] * parts,
            out_specs=IN_HBM,
            scratch_shapes=[
                pltpu.VMEM((TILES, parts, hidden, width // TILES), jnp.bfloat16),
                pltpu.VMEM(shape, jnp.bfloat16),
                pltpu.SemaphoreType.DMA((TILES, parts)),
                pltpu.SemaphoreType.DMA((TILES,)),
            ],
        ),
        out_shape=jax.ShapeDtypeStruct(shape, jnp.bfloat16),
        compiler_params=pltpu.CompilerParams(vmem_limit_bytes=60 * MIB),
        cost_estimate=pl.CostEstimate(
            flops=2 * rows * parts * hidden * width,
            bytes_accessed=2 * (parts * hidden * (rows + width) + rows * width),
            transcendentals=0,
        ),
        name="down",
    )(me, *acts, w_down, *pieces)


def place_kernel(spot_ref, rows_ref, *rest):
    out_ref, slots, departures = rest[-3:]
    tile = rows_ref.shape[1] // TILES
    leaving = []
    for number in range(TILES):
        where = pl.ds(number * tile, tile)
        total = lax.dot_general(
            spot_ref[...], rows_ref[:, where], (((0,), (0,)), ((), ())), preferred_element_type=jnp.float32
        )
        store_slots(slots.at[:, :, where], total)
        leaving.append(
            pltpu.make_async_copy(slots.at[:, :, where], out_ref.at[:, :, where], departures.at[number])
        )
        leaving[-1].start()
    for copy in leaving:
        copy.wait()


def wait_kernel(*refs):
    refs[-1][...] = jnp.zeros(refs[-1].shape, refs[-1].dtype)


def wait_for(arrays, told):
    return pl.pallas_call(
        wait_kernel,
        grid=(1,),
        in_specs=[CORNER if array.ndim == 2 else CORNER_SLOTS for array in arrays],
        out_specs=CORNER,
        out_shape=jax.ShapeDtypeStruct((16, 128), jnp.bfloat16),
        cost_estimate=pl.CostEstimate(flops=told, bytes_accessed=0, transcendentals=0),
        name="wait_for",
    )(*arrays)


def place_rows(spot, rows, experts, after, told):
    slots, width = spot.shape[1], rows.shape[1]
    shape = (experts, slots // experts, width)
    return pl.pallas_call(
        place_kernel,
        grid=(1,),
        in_specs=[
            pl.BlockSpec((rows.shape[0], slots), lambda i: (0, 0)),
            pl.BlockSpec((rows.shape[0], width), lambda i: (0, 0)),
        ]
        + [CORNER if array.ndim == 2 else CORNER_SLOTS for array in after],
        out_specs=IN_HBM,
        scratch_shapes=[pltpu.VMEM(shape, jnp.bfloat16), pltpu.SemaphoreType.DMA((TILES,))],
        out_shape=jax.ShapeDtypeStruct(shape, jnp.bfloat16),
        compiler_params=pltpu.CompilerParams(vmem_limit_bytes=60 * MIB),
        cost_estimate=pl.CostEstimate(
            flops=2 * slots * rows.shape[0] * width * told,
            bytes_accessed=2 * (slots + rows.shape[0]) * width,
            transcendentals=0,
        ),
        name="place_rows",
    )(spot, rows, *after)


def on_device(hidden_rows, expert_ids, affinity, w_gate, w_up, w_down):
    experts = lax.axis_size("ep")
    parts = lax.axis_size("tp")
    row_count, width = hidden_rows.shape
    place = lax.axis_index("tp")
    me = place.reshape(1).astype(jnp.int32)
    w_gate = w_gate[0].reshape(parts, width, w_gate.shape[2])
    w_up = w_up[0].reshape(parts, width, w_up.shape[2])
    w_down = w_down[0]

    def send(array, step):
        return lax.ppermute(array, "tp", [(i, (i + step) % parts) for i in range(parts)])

    def send_all(array):
        return [send(array, step) for step in SENDS]

    slices = [
        lax.dynamic_slice_in_dim(w_down, (place + step) % parts * width, width, axis=1) for step in SENDS
    ]
    pieces = [send(part, step) for part, step in zip(slices, SENDS)]

    route_weight = route_scale * affinity / jnp.sum(affinity, axis=1, keepdims=True)
    named = expert_ids[:, :, None] == jnp.arange(experts, dtype=jnp.int32)
    chosen = jnp.any(named, axis=1)
    weight = jnp.sum(jnp.where(named, route_weight[:, :, None], 0.0), axis=1)
    earlier = jnp.tril(jnp.ones((row_count, row_count), jnp.bfloat16), -1)
    slot = jnp.dot(earlier, chosen.astype(jnp.bfloat16), preferred_element_type=jnp.float32).astype(jnp.int32)
    slot = jnp.where(chosen, slot, CAP)

    places, gathered = [], []
    for number, (first, count, by_permutes) in enumerate(CHUNKS):
        here = slot[:, :, None] == first + jnp.arange(count, dtype=jnp.int32)
        places.append(here.reshape(row_count, experts * count))
        after = slices if number == 0 else [before] if number == 1 else [before, waited]
        outgoing = place_rows(places[-1].astype(jnp.bfloat16), hidden_rows, experts, after, 1)
        rows = lax.all_to_all(outgoing, "ep", split_axis=0, concat_axis=0, tiled=True)
        if number == 0:
            waited = wait_for([*pieces, rows], WAIT_TOLD)
        before = rows
        rows = rows.reshape(experts * count, width)
        gathered.append([rows] + send_all(rows) if by_permutes else lax.all_gather(rows, "tp"))

    mixed = jnp.zeros((row_count, width), jnp.float32)
    for number, ((first, count, by_permutes), spot, x, told) in enumerate(zip(CHUNKS, places, gathered, TOLD)):
        after = [activated] if number else []
        activated = hidden_units(me, x if by_permutes else [x], w_gate, w_up, after, told)
        outputs = down(me, [activated] + send_all(activated), w_down, pieces, experts)
        returned = lax.all_to_all(outputs, "ep", split_axis=0, concat_axis=0, tiled=True)
        returned = returned.reshape(experts * count, width)
        mix = jnp.where(spot, jnp.repeat(weight, count, axis=1), 0.0)
        high = mix.astype(jnp.bfloat16)
        low = (mix - high.astype(jnp.float32)).astype(jnp.bfloat16)
        mixed = mixed + jnp.dot(high, returned, preferred_element_type=jnp.float32)
        mixed = mixed + jnp.dot(low, returned, preferred_element_type=jnp.float32)
    return mixed.astype(jnp.bfloat16)


def solution(mesh):
    in_specs = (
        P("ep", "tp"),
        P("ep", None),
        P("ep", None),
        P("ep", None, "tp"),
        P("ep", None, "tp"),
        P("ep", "tp", None),
    )
    out_specs = P("ep", "tp")
    return jax.shard_map(
        on_device, mesh=mesh, in_specs=in_specs, out_specs=out_specs, check_vma=False
    )
```

```python
import functools

import jax
import jax.numpy as jnp
from jax import lax
from jax.experimental import pallas as pl
from jax.experimental.pallas import tpu as pltpu
from jax.sharding import PartitionSpec as P

CAP = 12
CHUNKS = ((0, 4, False), (4, 4, True), (8, 4, False))
SENDS = (1, 3, 2)
STEPS = (0, 3, 1, 2)
TILES = 2
TOLD = (100, 100, 1)
WAIT_TOLD = 200_000_000_000
MIB = 1024 * 1024
CORNER = pl.BlockSpec((16, 128), lambda *index: (0, 0))
IN_HBM = pl.BlockSpec(memory_space=pltpu.HBM)
CORNER_SLOTS = pl.BlockSpec((8, 4, 128), lambda *index: (0, 0, 0))


route_scale = 2.5


def store_slots(out_ref, total):
    count = out_ref.shape[1]
    for expert in range(out_ref.shape[0]):
        out_ref[expert] = total[expert * count:(expert + 1) * count].astype(out_ref.dtype)


def silu_times(gate, up):
    return gate / (1.0 + jnp.exp(-gate)) * up


def hidden_kernel(gathered, parts, me_ref, *refs):
    arrays = 1 if gathered else parts + 1
    xs, (gate_ref, up_ref) = refs[:arrays], refs[arrays:arrays + 2]
    out_ref, x_buffer, gate_buffer, up_buffer, gate_sum, up_sum, arrivals = refs[-7:]
    copies = []
    for number, step in enumerate(range(parts) if gathered else STEPS):
        part = step if gathered else lax.rem(me_ref[0] + step, parts)
        pairs = [(gate_ref.at[part], gate_buffer.at[number]), (up_ref.at[part], up_buffer.at[number])]
        if gathered:
            pairs.append((xs[0].at[step], x_buffer.at[number]))
        elif number < parts - 1:
            pairs.append((xs[number], x_buffer.at[number]))
        else:
            half = x_buffer.shape[1] // 2
            pairs.append((xs[number], x_buffer.at[number, pl.ds(0, half)]))
            pairs.append((xs[number + 1], x_buffer.at[number, pl.ds(half, half)]))
        copies.append(
            [pltpu.make_async_copy(a, b, arrivals.at[number, i]) for i, (a, b) in enumerate(pairs)]
        )
        for copy in copies[-1]:
            copy.start()
    for number in range(parts):
        for copy in copies[number]:
            copy.wait()
        x = x_buffer[number]
        gate_part = jnp.dot(x, gate_buffer[number], preferred_element_type=jnp.float32)
        up_part = jnp.dot(x, up_buffer[number], preferred_element_type=jnp.float32)
        if number == 0:
            gate_sum[...] = gate_part
            up_sum[...] = up_part
        elif number < parts - 1:
            gate_sum[...] += gate_part
            up_sum[...] += up_part
        else:
            out_ref[...] = silu_times(gate_sum[...] + gate_part, up_sum[...] + up_part).astype(out_ref.dtype)


def hidden_units(me, xs, w_gate, w_up, after, told):
    gathered = len(xs) == 1
    parts, width, hidden = w_gate.shape
    rows = xs[0].shape[-2]
    return pl.pallas_call(
        functools.partial(hidden_kernel, gathered, parts),
        grid_spec=pltpu.PrefetchScalarGridSpec(
            num_scalar_prefetch=1,
            grid=(1,),
            in_specs=[IN_HBM] * (len(xs) + 2) + [CORNER] * len(after),
            out_specs=pl.BlockSpec((rows, hidden), lambda i, me: (0, 0)),
            scratch_shapes=[
                pltpu.VMEM((parts, rows, width), jnp.bfloat16),
                pltpu.VMEM((parts, width, hidden), jnp.bfloat16),
                pltpu.VMEM((parts, width, hidden), jnp.bfloat16),
                pltpu.VMEM((rows, hidden), jnp.float32),
                pltpu.VMEM((rows, hidden), jnp.float32),
                pltpu.SemaphoreType.DMA((parts, 4)),
            ],
        ),
        out_shape=jax.ShapeDtypeStruct((rows, hidden), jnp.bfloat16),
        compiler_params=pltpu.CompilerParams(vmem_limit_bytes=60 * MIB),
        cost_estimate=pl.CostEstimate(
            flops=4 * rows * parts * width * hidden * told,
            bytes_accessed=2 * parts * width * (rows + 2 * hidden) + 2 * rows * hidden,
            transcendentals=rows * hidden,
        ),
        name="hidden_units",
    )(me, *xs, w_gate, w_up, *after)


def down_kernel(parts, me_ref, *refs):
    acts, own_ref, pieces = refs[:parts], refs[parts], refs[parts + 1:2 * parts]
    out_ref, weights, slots, arrivals, departures = refs[-5:]
    width = slots.shape[2]
    tile = width // TILES
    copies = []
    for number in range(TILES):
        sources = [own_ref.at[:, pl.ds(pl.multiple_of(me_ref[0] * width + number * tile, 128), tile)]]
        sources += [piece.at[:, pl.ds(number * tile, tile)] for piece in pieces]
        copies.append([
            pltpu.make_async_copy(source, weights.at[number, i], arrivals.at[number, i])
            for i, source in enumerate(sources)
        ])
        for copy in copies[-1]:
            copy.start()
    leaving = []
    for number in range(TILES):
        for copy in copies[number]:
            copy.wait()
        total = jnp.dot(acts[0][...], weights[number, 0], preferred_element_type=jnp.float32)
        for i in range(1, parts):
            total += jnp.dot(acts[i][...], weights[number, i], preferred_element_type=jnp.float32)
        store_slots(slots.at[:, :, pl.ds(number * tile, tile)], total)
        where = pl.ds(number * tile, tile)
        leaving.append(
            pltpu.make_async_copy(slots.at[:, :, where], out_ref.at[:, :, where], departures.at[number])
        )
        leaving[-1].start()
    for copy in leaving:
        copy.wait()


def down(me, acts, w_down, pieces, experts):
    rows, hidden = acts[0].shape
    width = pieces[0].shape[1]
    parts = len(acts)
    shape = (experts, rows // experts, width)
    return pl.pallas_call(
        functools.partial(down_kernel, parts),
        grid_spec=pltpu.PrefetchScalarGridSpec(
            num_scalar_prefetch=1,
            grid=(1,),
            in_specs=[pl.BlockSpec((rows, hidden), lambda i, me: (0, 0))] * parts + [IN_HBM] * parts,
            out_specs=IN_HBM,
            scratch_shapes=[
                pltpu.VMEM((TILES, parts, hidden, width // TILES), jnp.bfloat16),
                pltpu.VMEM(shape, jnp.bfloat16),
                pltpu.SemaphoreType.DMA((TILES, parts)),
                pltpu.SemaphoreType.DMA((TILES,)),
            ],
        ),
        out_shape=jax.ShapeDtypeStruct(shape, jnp.bfloat16),
        compiler_params=pltpu.CompilerParams(vmem_limit_bytes=60 * MIB),
        cost_estimate=pl.CostEstimate(
            flops=2 * rows * parts * hidden * width,
            bytes_accessed=2 * (parts * hidden * (rows + width) + rows * width),
            transcendentals=0,
        ),
        name="down",
    )(me, *acts, w_down, *pieces)


def place_kernel(spot_ref, rows_ref, *rest):
    out_ref, slots, departures = rest[-3:]
    tile = rows_ref.shape[1] // TILES
    leaving = []
    for number in range(TILES):
        where = pl.ds(number * tile, tile)
        total = lax.dot_general(
            spot_ref[...], rows_ref[:, where], (((0,), (0,)), ((), ())), preferred_element_type=jnp.float32
        )
        store_slots(slots.at[:, :, where], total)
        leaving.append(
            pltpu.make_async_copy(slots.at[:, :, where], out_ref.at[:, :, where], departures.at[number])
        )
        leaving[-1].start()
    for copy in leaving:
        copy.wait()


def wait_kernel(*refs):
    refs[-1][...] = jnp.zeros(refs[-1].shape, refs[-1].dtype)


def wait_for(arrays, told):
    return pl.pallas_call(
        wait_kernel,
        grid=(1,),
        in_specs=[CORNER if array.ndim == 2 else CORNER_SLOTS for array in arrays],
        out_specs=CORNER,
        out_shape=jax.ShapeDtypeStruct((16, 128), jnp.bfloat16),
        cost_estimate=pl.CostEstimate(flops=told, bytes_accessed=0, transcendentals=0),
        name="wait_for",
    )(*arrays)


def place_rows(spot, rows, experts, after, told):
    slots, width = spot.shape[1], rows.shape[1]
    shape = (experts, slots // experts, width)
    return pl.pallas_call(
        place_kernel,
        grid=(1,),
        in_specs=[
            pl.BlockSpec((rows.shape[0], slots), lambda i: (0, 0)),
            pl.BlockSpec((rows.shape[0], width), lambda i: (0, 0)),
        ]
        + [CORNER if array.ndim == 2 else CORNER_SLOTS for array in after],
        out_specs=IN_HBM,
        scratch_shapes=[pltpu.VMEM(shape, jnp.bfloat16), pltpu.SemaphoreType.DMA((TILES,))],
        out_shape=jax.ShapeDtypeStruct(shape, jnp.bfloat16),
        compiler_params=pltpu.CompilerParams(vmem_limit_bytes=60 * MIB),
        cost_estimate=pl.CostEstimate(
            flops=2 * slots * rows.shape[0] * width * told,
            bytes_accessed=2 * (slots + rows.shape[0]) * width,
            transcendentals=0,
        ),
        name="place_rows",
    )(spot, rows, *after)


def on_device(hidden_rows, expert_ids, affinity, w_gate, w_up, w_down):
    experts = lax.axis_size("ep")
    parts = lax.axis_size("tp")
    row_count, width = hidden_rows.shape
    place = lax.axis_index("tp")
    me = place.reshape(1).astype(jnp.int32)
    w_gate = w_gate[0].reshape(parts, width, w_gate.shape[2])
    w_up = w_up[0].reshape(parts, width, w_up.shape[2])
    w_down = w_down[0]

    def send(array, step):
        return lax.ppermute(array, "tp", [(i, (i + step) % parts) for i in range(parts)])

    def send_all(array):
        return [send(array, step) for step in SENDS]

    def ring(rows):
        half = rows.shape[0] // 2
        left, right = send(rows, 1), send(rows, -1)
        return [left, right, send(left[:half], 1), send(right[half:], -1)]

    slices = [
        lax.dynamic_slice_in_dim(w_down, (place + step) % parts * width, width, axis=1) for step in SENDS
    ]
    pieces = [send(part, step) for part, step in zip(slices, SENDS)]

    route_weight = route_scale * affinity / jnp.sum(affinity, axis=1, keepdims=True)
    named = expert_ids[:, :, None] == jnp.arange(experts, dtype=jnp.int32)
    chosen = jnp.any(named, axis=1)
    weight = jnp.sum(jnp.where(named, route_weight[:, :, None], 0.0), axis=1)
    earlier = jnp.tril(jnp.ones((row_count, row_count), jnp.bfloat16), -1)
    slot = jnp.dot(earlier, chosen.astype(jnp.bfloat16), preferred_element_type=jnp.float32).astype(jnp.int32)
    slot = jnp.where(chosen, slot, CAP)

    places = []
    for first, count, _ in CHUNKS:
        here = slot[:, :, None] == first + jnp.arange(count, dtype=jnp.int32)
        places.append(here.reshape(row_count, experts * count))

    def outgoing(number, after):
        return place_rows(places[number].astype(jnp.bfloat16), hidden_rows, experts, after, 1)

    gathered = []
    leaving = [outgoing(0, []), None, None]
    leaving[2] = outgoing(2, leaving[:1])
    for number, (first, count, by_permutes) in enumerate(CHUNKS):
        if number == 1:
            leaving[1] = outgoing(1, [rows, leaving[2], wait_for(pieces, WAIT_TOLD)])
        rows = lax.all_to_all(leaving[number], "ep", split_axis=0, concat_axis=0, tiled=True)
        rows = rows.reshape(experts * count, width)
        if number == 1:
            waited = wait_for([rows], WAIT_TOLD)
        if by_permutes:
            gathered.append([rows] + ring(rows))
        else:
            gathered.append([lax.all_gather(rows, "tp", tiled=True).reshape(parts, *rows.shape)])

    mixed = jnp.zeros((row_count, width), jnp.float32)
    for number, ((first, count, by_permutes), spot, x, told) in enumerate(zip(CHUNKS, places, gathered, TOLD)):
        after = [activated] if number else [waited]
        activated = hidden_units(me, x, w_gate, w_up, after, told)
        outputs = down(me, [activated] + send_all(activated), w_down, pieces, experts)
        returned = lax.all_to_all(outputs, "ep", split_axis=0, concat_axis=0, tiled=True)
        returned = returned.reshape(experts * count, width)
        mix = jnp.where(spot, jnp.repeat(weight, count, axis=1), 0.0)
        high = mix.astype(jnp.bfloat16)
        low = (mix - high.astype(jnp.float32)).astype(jnp.bfloat16)
        mixed = mixed + jnp.dot(high, returned, preferred_element_type=jnp.float32)
        mixed = mixed + jnp.dot(low, returned, preferred_element_type=jnp.float32)
    return mixed.astype(jnp.bfloat16)


def solution(mesh):
    in_specs = (
        P("ep", "tp"),
        P("ep", None),
        P("ep", None),
        P("ep", None, "tp"),
        P("ep", None, "tp"),
        P("ep", "tp", None),
    )
    out_specs = P("ep", "tp")
    return jax.shard_map(
        on_device, mesh=mesh, in_specs=in_specs, out_specs=out_specs, check_vma=False
    )
```

```python
import functools

import jax
import jax.numpy as jnp
from jax import lax
from jax.experimental import pallas as pl
from jax.experimental.pallas import tpu as pltpu
from jax.sharding import PartitionSpec as P

CAP = 12
CHUNKS = ((0, 4, True), (4, 4, False), (8, 4, False))
SENDS = (1, 3, 2)
STEPS = (0, 3, 1, 2)
TILES = 2
TOLD = (100, 100, 1)
WAIT_TOLD = 200_000_000_000
MIB = 1024 * 1024
CORNER = pl.BlockSpec((16, 128), lambda *index: (0, 0))
IN_HBM = pl.BlockSpec(memory_space=pltpu.HBM)
CORNER_SLOTS = pl.BlockSpec((8, 4, 128), lambda *index: (0, 0, 0))


route_scale = 2.5


def store_slots(out_ref, total):
    count = out_ref.shape[1]
    for expert in range(out_ref.shape[0]):
        out_ref[expert] = total[expert * count:(expert + 1) * count].astype(out_ref.dtype)


def silu_times(gate, up):
    return gate / (1.0 + jnp.exp(-gate)) * up


def hidden_kernel(gathered, parts, me_ref, *refs):
    arrays = 1 if gathered else parts + 1
    xs, (gate_ref, up_ref) = refs[:arrays], refs[arrays:arrays + 2]
    out_ref, x_buffer, gate_buffer, up_buffer, gate_sum, up_sum, arrivals = refs[-7:]
    copies = []
    for number, step in enumerate(range(parts) if gathered else STEPS):
        part = step if gathered else lax.rem(me_ref[0] + step, parts)
        pairs = [(gate_ref.at[part], gate_buffer.at[number]), (up_ref.at[part], up_buffer.at[number])]
        if gathered:
            pairs.append((xs[0].at[step], x_buffer.at[number]))
        elif number < parts - 1:
            pairs.append((xs[number], x_buffer.at[number]))
        else:
            half = x_buffer.shape[1] // 2
            pairs.append((xs[number], x_buffer.at[number, pl.ds(0, half)]))
            pairs.append((xs[number + 1], x_buffer.at[number, pl.ds(half, half)]))
        copies.append(
            [pltpu.make_async_copy(a, b, arrivals.at[number, i]) for i, (a, b) in enumerate(pairs)]
        )
        for copy in copies[-1]:
            copy.start()
    for number in range(parts):
        for copy in copies[number]:
            copy.wait()
        x = x_buffer[number]
        gate_part = jnp.dot(x, gate_buffer[number], preferred_element_type=jnp.float32)
        up_part = jnp.dot(x, up_buffer[number], preferred_element_type=jnp.float32)
        if number == 0:
            gate_sum[...] = gate_part
            up_sum[...] = up_part
        elif number < parts - 1:
            gate_sum[...] += gate_part
            up_sum[...] += up_part
        else:
            out_ref[...] = silu_times(gate_sum[...] + gate_part, up_sum[...] + up_part).astype(out_ref.dtype)


def hidden_units(me, xs, w_gate, w_up, after, told):
    gathered = len(xs) == 1
    parts, width, hidden = w_gate.shape
    rows = xs[0].shape[-2]
    return pl.pallas_call(
        functools.partial(hidden_kernel, gathered, parts),
        grid_spec=pltpu.PrefetchScalarGridSpec(
            num_scalar_prefetch=1,
            grid=(1,),
            in_specs=[IN_HBM] * (len(xs) + 2) + [CORNER] * len(after),
            out_specs=pl.BlockSpec((rows, hidden), lambda i, me: (0, 0)),
            scratch_shapes=[
                pltpu.VMEM((parts, rows, width), jnp.bfloat16),
                pltpu.VMEM((parts, width, hidden), jnp.bfloat16),
                pltpu.VMEM((parts, width, hidden), jnp.bfloat16),
                pltpu.VMEM((rows, hidden), jnp.float32),
                pltpu.VMEM((rows, hidden), jnp.float32),
                pltpu.SemaphoreType.DMA((parts, 4)),
            ],
        ),
        out_shape=jax.ShapeDtypeStruct((rows, hidden), jnp.bfloat16),
        compiler_params=pltpu.CompilerParams(vmem_limit_bytes=60 * MIB),
        cost_estimate=pl.CostEstimate(
            flops=4 * rows * parts * width * hidden * told,
            bytes_accessed=2 * parts * width * (rows + 2 * hidden) + 2 * rows * hidden,
            transcendentals=rows * hidden,
        ),
        name="hidden_units",
    )(me, *xs, w_gate, w_up, *after)


def down_kernel(parts, me_ref, *refs):
    acts, own_ref, pieces = refs[:parts], refs[parts], refs[parts + 1:2 * parts]
    out_ref, weights, slots, arrivals, departures = refs[-5:]
    width = slots.shape[2]
    tile = width // TILES
    copies = []
    for number in range(TILES):
        sources = [own_ref.at[:, pl.ds(pl.multiple_of(me_ref[0] * width + number * tile, 128), tile)]]
        sources += [piece.at[:, pl.ds(number * tile, tile)] for piece in pieces]
        copies.append([
            pltpu.make_async_copy(source, weights.at[number, i], arrivals.at[number, i])
            for i, source in enumerate(sources)
        ])
        for copy in copies[-1]:
            copy.start()
    leaving = []
    for number in range(TILES):
        for copy in copies[number]:
            copy.wait()
        total = jnp.dot(acts[0][...], weights[number, 0], preferred_element_type=jnp.float32)
        for i in range(1, parts):
            total += jnp.dot(acts[i][...], weights[number, i], preferred_element_type=jnp.float32)
        store_slots(slots.at[:, :, pl.ds(number * tile, tile)], total)
        where = pl.ds(number * tile, tile)
        leaving.append(
            pltpu.make_async_copy(slots.at[:, :, where], out_ref.at[:, :, where], departures.at[number])
        )
        leaving[-1].start()
    for copy in leaving:
        copy.wait()


def down(me, acts, w_down, pieces, experts):
    rows, hidden = acts[0].shape
    width = pieces[0].shape[1]
    parts = len(acts)
    shape = (experts, rows // experts, width)
    return pl.pallas_call(
        functools.partial(down_kernel, parts),
        grid_spec=pltpu.PrefetchScalarGridSpec(
            num_scalar_prefetch=1,
            grid=(1,),
            in_specs=[pl.BlockSpec((rows, hidden), lambda i, me: (0, 0))] * parts + [IN_HBM] * parts,
            out_specs=IN_HBM,
            scratch_shapes=[
                pltpu.VMEM((TILES, parts, hidden, width // TILES), jnp.bfloat16),
                pltpu.VMEM(shape, jnp.bfloat16),
                pltpu.SemaphoreType.DMA((TILES, parts)),
                pltpu.SemaphoreType.DMA((TILES,)),
            ],
        ),
        out_shape=jax.ShapeDtypeStruct(shape, jnp.bfloat16),
        compiler_params=pltpu.CompilerParams(vmem_limit_bytes=60 * MIB),
        cost_estimate=pl.CostEstimate(
            flops=2 * rows * parts * hidden * width,
            bytes_accessed=2 * (parts * hidden * (rows + width) + rows * width),
            transcendentals=0,
        ),
        name="down",
    )(me, *acts, w_down, *pieces)


def place_kernel(spot_ref, rows_ref, *rest):
    out_ref, slots, departures = rest[-3:]
    tile = rows_ref.shape[1] // TILES
    leaving = []
    for number in range(TILES):
        where = pl.ds(number * tile, tile)
        total = lax.dot_general(
            spot_ref[...], rows_ref[:, where], (((0,), (0,)), ((), ())), preferred_element_type=jnp.float32
        )
        store_slots(slots.at[:, :, where], total)
        leaving.append(
            pltpu.make_async_copy(slots.at[:, :, where], out_ref.at[:, :, where], departures.at[number])
        )
        leaving[-1].start()
    for copy in leaving:
        copy.wait()


def wait_kernel(*refs):
    refs[-1][...] = jnp.zeros(refs[-1].shape, refs[-1].dtype)


def wait_for(arrays, told):
    return pl.pallas_call(
        wait_kernel,
        grid=(1,),
        in_specs=[CORNER if array.ndim == 2 else CORNER_SLOTS for array in arrays],
        out_specs=CORNER,
        out_shape=jax.ShapeDtypeStruct((16, 128), jnp.bfloat16),
        cost_estimate=pl.CostEstimate(flops=told, bytes_accessed=0, transcendentals=0),
        name="wait_for",
    )(*arrays)


def place_rows(spot, rows, experts, after, told):
    slots, width = spot.shape[1], rows.shape[1]
    shape = (experts, slots // experts, width)
    return pl.pallas_call(
        place_kernel,
        grid=(1,),
        in_specs=[
            pl.BlockSpec((rows.shape[0], slots), lambda i: (0, 0)),
            pl.BlockSpec((rows.shape[0], width), lambda i: (0, 0)),
        ]
        + [CORNER if array.ndim == 2 else CORNER_SLOTS for array in after],
        out_specs=IN_HBM,
        scratch_shapes=[pltpu.VMEM(shape, jnp.bfloat16), pltpu.SemaphoreType.DMA((TILES,))],
        out_shape=jax.ShapeDtypeStruct(shape, jnp.bfloat16),
        compiler_params=pltpu.CompilerParams(vmem_limit_bytes=60 * MIB),
        cost_estimate=pl.CostEstimate(
            flops=2 * slots * rows.shape[0] * width * told,
            bytes_accessed=2 * (slots + rows.shape[0]) * width,
            transcendentals=0,
        ),
        name="place_rows",
    )(spot, rows, *after)


def on_device(hidden_rows, expert_ids, affinity, w_gate, w_up, w_down):
    experts = lax.axis_size("ep")
    parts = lax.axis_size("tp")
    row_count, width = hidden_rows.shape
    place = lax.axis_index("tp")
    me = place.reshape(1).astype(jnp.int32)
    w_gate = w_gate[0].reshape(parts, width, w_gate.shape[2])
    w_up = w_up[0].reshape(parts, width, w_up.shape[2])
    w_down = w_down[0]

    def send(array, step):
        return lax.ppermute(array, "tp", [(i, (i + step) % parts) for i in range(parts)])

    def send_all(array):
        return [send(array, step) for step in SENDS]

    def ring(rows):
        half = rows.shape[0] // 2
        left, right = send(rows, 1), send(rows, -1)
        return [left, right, send(left[:half], 1), send(right[half:], -1)]

    slices = [
        lax.dynamic_slice_in_dim(w_down, (place + step) % parts * width, width, axis=1) for step in SENDS
    ]
    pieces = [send(part, step) for part, step in zip(slices, SENDS)]

    route_weight = route_scale * affinity / jnp.sum(affinity, axis=1, keepdims=True)
    named = expert_ids[:, :, None] == jnp.arange(experts, dtype=jnp.int32)
    chosen = jnp.any(named, axis=1)
    weight = jnp.sum(jnp.where(named, route_weight[:, :, None], 0.0), axis=1)
    earlier = jnp.tril(jnp.ones((row_count, row_count), jnp.bfloat16), -1)
    slot = jnp.dot(earlier, chosen.astype(jnp.bfloat16), preferred_element_type=jnp.float32).astype(jnp.int32)
    slot = jnp.where(chosen, slot, CAP)

    places = []
    for first, count, _ in CHUNKS:
        here = slot[:, :, None] == first + jnp.arange(count, dtype=jnp.int32)
        places.append(here.reshape(row_count, experts * count))

    def outgoing(number, after):
        return place_rows(places[number].astype(jnp.bfloat16), hidden_rows, experts, after, 1)

    gathered = []
    leaving = [outgoing(0, []), None, None]
    leaving[2] = outgoing(2, leaving[:1])
    for number, (first, count, by_permutes) in enumerate(CHUNKS):
        if number == 1:
            leaving[1] = outgoing(1, [rows, leaving[2], wait_for(pieces, WAIT_TOLD)])
        rows = lax.all_to_all(leaving[number], "ep", split_axis=0, concat_axis=0, tiled=True)
        rows = rows.reshape(experts * count, width)
        if number == 1:
            waited = wait_for([rows], WAIT_TOLD)
        if by_permutes:
            gathered.append([rows] + ring(rows))
        else:
            gathered.append([lax.all_gather(rows, "tp", tiled=True).reshape(parts, *rows.shape)])

    mixed = jnp.zeros((row_count, width), jnp.float32)
    for number, ((first, count, by_permutes), spot, x, told) in enumerate(zip(CHUNKS, places, gathered, TOLD)):
        after = [activated] if number else [waited]
        activated = hidden_units(me, x, w_gate, w_up, after, told)
        outputs = down(me, [activated] + send_all(activated), w_down, pieces, experts)
        returned = lax.all_to_all(outputs, "ep", split_axis=0, concat_axis=0, tiled=True)
        returned = returned.reshape(experts * count, width)
        mix = jnp.where(spot, jnp.repeat(weight, count, axis=1), 0.0)
        high = mix.astype(jnp.bfloat16)
        low = (mix - high.astype(jnp.float32)).astype(jnp.bfloat16)
        mixed = mixed + jnp.dot(high, returned, preferred_element_type=jnp.float32)
        mixed = mixed + jnp.dot(low, returned, preferred_element_type=jnp.float32)
    return mixed.astype(jnp.bfloat16)


def solution(mesh):
    in_specs = (
        P("ep", "tp"),
        P("ep", None),
        P("ep", None),
        P("ep", None, "tp"),
        P("ep", None, "tp"),
        P("ep", "tp", None),
    )
    out_specs = P("ep", "tp")
    return jax.shard_map(
        on_device, mesh=mesh, in_specs=in_specs, out_specs=out_specs, check_vma=False
    )
```

```python
import functools

import jax
import jax.numpy as jnp
from jax import lax
from jax.experimental import pallas as pl
from jax.experimental.pallas import tpu as pltpu
from jax.sharding import PartitionSpec as P

CAP = 12
DISPATCHES = ((0, 8), (8, 4))
CHUNKS = ((0, 4), (4, 4), (8, 4))
BY_RING = (False, True, False)
SENDS = (1, 3, 2)
STEPS = (0, 3, 1, 2)
TILES = 2
TOLD = (100, 10, 1)
WAIT_TOLD = 200_000_000_000
MIB = 1024 * 1024
CORNER = pl.BlockSpec((16, 128), lambda *index: (0, 0))
IN_HBM = pl.BlockSpec(memory_space=pltpu.HBM)
CORNER_SLOTS = pl.BlockSpec((8, 4, 128), lambda *index: (0, 0, 0))


route_scale = 2.5


def store_slots(out_ref, total):
    count = out_ref.shape[1]
    for expert in range(out_ref.shape[0]):
        out_ref[expert] = total[expert * count:(expert + 1) * count].astype(out_ref.dtype)


def silu_times(gate, up):
    return gate / (1.0 + jnp.exp(-gate)) * up


def hidden_kernel(gathered, parts, me_ref, *refs):
    arrays = 1 if gathered else parts + 1
    xs, (gate_ref, up_ref) = refs[:arrays], refs[arrays:arrays + 2]
    out_ref, x_buffer, gate_buffer, up_buffer, gate_sum, up_sum, arrivals = refs[-7:]
    copies = []
    for number, step in enumerate(range(parts) if gathered else STEPS):
        part = step if gathered else lax.rem(me_ref[0] + step, parts)
        pairs = [(gate_ref.at[part], gate_buffer.at[number]), (up_ref.at[part], up_buffer.at[number])]
        if gathered:
            pairs.append((xs[0].at[step], x_buffer.at[number]))
        elif number < parts - 1:
            pairs.append((xs[number], x_buffer.at[number]))
        else:
            half = x_buffer.shape[1] // 2
            pairs.append((xs[number], x_buffer.at[number, pl.ds(0, half)]))
            pairs.append((xs[number + 1], x_buffer.at[number, pl.ds(half, half)]))
        copies.append(
            [pltpu.make_async_copy(a, b, arrivals.at[number, i]) for i, (a, b) in enumerate(pairs)]
        )
        for copy in copies[-1]:
            copy.start()
    for number in range(parts):
        for copy in copies[number]:
            copy.wait()
        x = x_buffer[number]
        gate_part = jnp.dot(x, gate_buffer[number], preferred_element_type=jnp.float32)
        up_part = jnp.dot(x, up_buffer[number], preferred_element_type=jnp.float32)
        if number == 0:
            gate_sum[...] = gate_part
            up_sum[...] = up_part
        elif number < parts - 1:
            gate_sum[...] += gate_part
            up_sum[...] += up_part
        else:
            out_ref[...] = silu_times(gate_sum[...] + gate_part, up_sum[...] + up_part).astype(out_ref.dtype)


def hidden_units(me, xs, w_gate, w_up, after, told):
    gathered = len(xs) == 1
    parts, width, hidden = w_gate.shape
    rows = xs[0].shape[-2]
    return pl.pallas_call(
        functools.partial(hidden_kernel, gathered, parts),
        grid_spec=pltpu.PrefetchScalarGridSpec(
            num_scalar_prefetch=1,
            grid=(1,),
            in_specs=[IN_HBM] * (len(xs) + 2) + [CORNER] * len(after),
            out_specs=pl.BlockSpec((rows, hidden), lambda i, me: (0, 0)),
            scratch_shapes=[
                pltpu.VMEM((parts, rows, width), jnp.bfloat16),
                pltpu.VMEM((parts, width, hidden), jnp.bfloat16),
                pltpu.VMEM((parts, width, hidden), jnp.bfloat16),
                pltpu.VMEM((rows, hidden), jnp.float32),
                pltpu.VMEM((rows, hidden), jnp.float32),
                pltpu.SemaphoreType.DMA((parts, 4)),
            ],
        ),
        out_shape=jax.ShapeDtypeStruct((rows, hidden), jnp.bfloat16),
        compiler_params=pltpu.CompilerParams(vmem_limit_bytes=60 * MIB),
        cost_estimate=pl.CostEstimate(
            flops=4 * rows * parts * width * hidden * told,
            bytes_accessed=2 * parts * width * (rows + 2 * hidden) + 2 * rows * hidden,
            transcendentals=rows * hidden,
        ),
        name="hidden_units",
    )(me, *xs, w_gate, w_up, *after)


def down_kernel(parts, me_ref, *refs):
    acts, own_ref, pieces = refs[:parts], refs[parts], refs[parts + 1:2 * parts]
    out_ref, weights, slots, arrivals, departures = refs[-5:]
    width = slots.shape[2]
    tile = width // TILES
    copies = []
    for number in range(TILES):
        sources = [own_ref.at[:, pl.ds(pl.multiple_of(me_ref[0] * width + number * tile, 128), tile)]]
        sources += [piece.at[:, pl.ds(number * tile, tile)] for piece in pieces]
        copies.append([
            pltpu.make_async_copy(source, weights.at[number, i], arrivals.at[number, i])
            for i, source in enumerate(sources)
        ])
        for copy in copies[-1]:
            copy.start()
    leaving = []
    for number in range(TILES):
        for copy in copies[number]:
            copy.wait()
        total = jnp.dot(acts[0][...], weights[number, 0], preferred_element_type=jnp.float32)
        for i in range(1, parts):
            total += jnp.dot(acts[i][...], weights[number, i], preferred_element_type=jnp.float32)
        store_slots(slots.at[:, :, pl.ds(number * tile, tile)], total)
        where = pl.ds(number * tile, tile)
        leaving.append(
            pltpu.make_async_copy(slots.at[:, :, where], out_ref.at[:, :, where], departures.at[number])
        )
        leaving[-1].start()
    for copy in leaving:
        copy.wait()


def down(me, acts, w_down, pieces, experts):
    rows, hidden = acts[0].shape
    width = pieces[0].shape[1]
    parts = len(acts)
    shape = (experts, rows // experts, width)
    return pl.pallas_call(
        functools.partial(down_kernel, parts),
        grid_spec=pltpu.PrefetchScalarGridSpec(
            num_scalar_prefetch=1,
            grid=(1,),
            in_specs=[pl.BlockSpec((rows, hidden), lambda i, me: (0, 0))] * parts + [IN_HBM] * parts,
            out_specs=IN_HBM,
            scratch_shapes=[
                pltpu.VMEM((TILES, parts, hidden, width // TILES), jnp.bfloat16),
                pltpu.VMEM(shape, jnp.bfloat16),
                pltpu.SemaphoreType.DMA((TILES, parts)),
                pltpu.SemaphoreType.DMA((TILES,)),
            ],
        ),
        out_shape=jax.ShapeDtypeStruct(shape, jnp.bfloat16),
        compiler_params=pltpu.CompilerParams(vmem_limit_bytes=60 * MIB),
        cost_estimate=pl.CostEstimate(
            flops=2 * rows * parts * hidden * width,
            bytes_accessed=2 * (parts * hidden * (rows + width) + rows * width),
            transcendentals=0,
        ),
        name="down",
    )(me, *acts, w_down, *pieces)


def place_kernel(spot_ref, rows_ref, *rest):
    out_ref, slots, departures = rest[-3:]
    tile = rows_ref.shape[1] // TILES
    leaving = []
    for number in range(TILES):
        where = pl.ds(number * tile, tile)
        total = lax.dot_general(
            spot_ref[...], rows_ref[:, where], (((0,), (0,)), ((), ())), preferred_element_type=jnp.float32
        )
        store_slots(slots.at[:, :, where], total)
        leaving.append(
            pltpu.make_async_copy(slots.at[:, :, where], out_ref.at[:, :, where], departures.at[number])
        )
        leaving[-1].start()
    for copy in leaving:
        copy.wait()


def wait_kernel(*refs):
    refs[-1][...] = jnp.zeros(refs[-1].shape, refs[-1].dtype)


def wait_for(arrays, told):
    return pl.pallas_call(
        wait_kernel,
        grid=(1,),
        in_specs=[CORNER if array.ndim == 2 else CORNER_SLOTS for array in arrays],
        out_specs=CORNER,
        out_shape=jax.ShapeDtypeStruct((16, 128), jnp.bfloat16),
        cost_estimate=pl.CostEstimate(flops=told, bytes_accessed=0, transcendentals=0),
        name="wait_for",
    )(*arrays)


def place_rows(spot, rows, experts, after, told):
    slots, width = spot.shape[1], rows.shape[1]
    shape = (experts, slots // experts, width)
    return pl.pallas_call(
        place_kernel,
        grid=(1,),
        in_specs=[
            pl.BlockSpec((rows.shape[0], slots), lambda i: (0, 0)),
            pl.BlockSpec((rows.shape[0], width), lambda i: (0, 0)),
        ]
        + [CORNER if array.ndim == 2 else CORNER_SLOTS for array in after],
        out_specs=IN_HBM,
        scratch_shapes=[pltpu.VMEM(shape, jnp.bfloat16), pltpu.SemaphoreType.DMA((TILES,))],
        out_shape=jax.ShapeDtypeStruct(shape, jnp.bfloat16),
        compiler_params=pltpu.CompilerParams(vmem_limit_bytes=60 * MIB),
        cost_estimate=pl.CostEstimate(
            flops=2 * slots * rows.shape[0] * width * told,
            bytes_accessed=2 * (slots + rows.shape[0]) * width,
            transcendentals=0,
        ),
        name="place_rows",
    )(spot, rows, *after)


def on_device(hidden_rows, expert_ids, affinity, w_gate, w_up, w_down):
    experts = lax.axis_size("ep")
    parts = lax.axis_size("tp")
    row_count, width = hidden_rows.shape
    place = lax.axis_index("tp")
    me = place.reshape(1).astype(jnp.int32)
    w_gate = w_gate[0].reshape(parts, width, w_gate.shape[2])
    w_up = w_up[0].reshape(parts, width, w_up.shape[2])
    w_down = w_down[0]

    def send(array, step):
        return lax.ppermute(array, "tp", [(i, (i + step) % parts) for i in range(parts)])

    def send_all(array):
        return [send(array, step) for step in SENDS]

    def ring(rows):
        half = rows.shape[0] // 2
        left, right = send(rows, 1), send(rows, -1)
        return [left, right, send(left[:half], 1), send(right[half:], -1)]

    slices = [
        lax.dynamic_slice_in_dim(w_down, (place + step) % parts * width, width, axis=1) for step in SENDS
    ]
    pieces = [send(part, step) for part, step in zip(slices, SENDS)]

    route_weight = route_scale * affinity / jnp.sum(affinity, axis=1, keepdims=True)
    named = expert_ids[:, :, None] == jnp.arange(experts, dtype=jnp.int32)
    chosen = jnp.any(named, axis=1)
    weight = jnp.sum(jnp.where(named, route_weight[:, :, None], 0.0), axis=1)
    earlier = jnp.tril(jnp.ones((row_count, row_count), jnp.bfloat16), -1)
    slot = jnp.dot(earlier, chosen.astype(jnp.bfloat16), preferred_element_type=jnp.float32).astype(jnp.int32)
    slot = jnp.where(chosen, slot, CAP)

    def spots(first, count):
        here = slot[:, :, None] == first + jnp.arange(count, dtype=jnp.int32)
        return here.reshape(row_count, experts * count)

    arrived = []
    for number, (first, count) in enumerate(DISPATCHES):
        after = [] if number == 0 else [arrived[0], wait_for(pieces, WAIT_TOLD)]
        spot = spots(first, count).astype(jnp.bfloat16)
        outgoing = place_rows(spot, hidden_rows, experts, after, 1)
        rows = lax.all_to_all(outgoing, "ep", split_axis=0, concat_axis=0, tiled=True)
        for start in range(0, count, 4):
            arrived.append(rows[:, start:start + 4].reshape(experts * 4, width))

    gathered = []
    for rows, by_ring in zip(arrived, BY_RING):
        if by_ring:
            gathered.append([rows] + ring(rows))
        else:
            gathered.append([lax.all_gather(rows, "tp", tiled=True).reshape(parts, *rows.shape)])

    mixed = jnp.zeros((row_count, width), jnp.float32)
    for number, ((first, count), x, told) in enumerate(zip(CHUNKS, gathered, TOLD)):
        after = [activated] if number else []
        activated = hidden_units(me, x, w_gate, w_up, after, told)
        outputs = down(me, [activated] + send_all(activated), w_down, pieces, experts)
        returned = lax.all_to_all(outputs, "ep", split_axis=0, concat_axis=0, tiled=True)
        returned = returned.reshape(experts * count, width)
        mix = jnp.where(spots(first, count), jnp.repeat(weight, count, axis=1), 0.0)
        high = mix.astype(jnp.bfloat16)
        low = (mix - high.astype(jnp.float32)).astype(jnp.bfloat16)
        mixed = mixed + jnp.dot(high, returned, preferred_element_type=jnp.float32)
        mixed = mixed + jnp.dot(low, returned, preferred_element_type=jnp.float32)
    return mixed.astype(jnp.bfloat16)


def solution(mesh):
    in_specs = (
        P("ep", "tp"),
        P("ep", None),
        P("ep", None),
        P("ep", None, "tp"),
        P("ep", None, "tp"),
        P("ep", "tp", None),
    )
    out_specs = P("ep", "tp")
    return jax.shard_map(
        on_device, mesh=mesh, in_specs=in_specs, out_specs=out_specs, check_vma=False
    )
```

```python
import functools

import jax
import jax.numpy as jnp
from jax import lax
from jax.experimental import pallas as pl
from jax.experimental.pallas import tpu as pltpu
from jax.sharding import PartitionSpec as P

CAP = 12
CHUNKS = ((0, 4, False), (4, 4, False), (8, 4, False))
SENDS = (1, 3, 2)
STEPS = (0, 3, 1, 2)
TILES = 2
TOLD = (1000, 100, 1)
WAIT_TOLD = 200_000_000_000
MIB = 1024 * 1024
CORNER = pl.BlockSpec((16, 128), lambda *index: (0, 0))
IN_HBM = pl.BlockSpec(memory_space=pltpu.HBM)
CORNER_SLOTS = pl.BlockSpec((8, 4, 128), lambda *index: (0, 0, 0))


route_scale = 2.5


def store_slots(out_ref, total):
    count = out_ref.shape[1]
    for expert in range(out_ref.shape[0]):
        out_ref[expert] = total[expert * count:(expert + 1) * count].astype(out_ref.dtype)


def silu_times(gate, up):
    return gate / (1.0 + jnp.exp(-gate)) * up


def hidden_kernel(gathered, parts, me_ref, *refs):
    arrays = 1 if gathered else parts + 1
    xs, (gate_ref, up_ref) = refs[:arrays], refs[arrays:arrays + 2]
    out_ref, x_buffer, gate_buffer, up_buffer, gate_sum, up_sum, arrivals = refs[-7:]
    copies = []
    for number, step in enumerate(range(parts) if gathered else STEPS):
        part = step if gathered else lax.rem(me_ref[0] + step, parts)
        pairs = [(gate_ref.at[part], gate_buffer.at[number]), (up_ref.at[part], up_buffer.at[number])]
        if gathered:
            pairs.append((xs[0].at[step], x_buffer.at[number]))
        elif number < parts - 1:
            pairs.append((xs[number], x_buffer.at[number]))
        else:
            half = x_buffer.shape[1] // 2
            pairs.append((xs[number], x_buffer.at[number, pl.ds(0, half)]))
            pairs.append((xs[number + 1], x_buffer.at[number, pl.ds(half, half)]))
        copies.append(
            [pltpu.make_async_copy(a, b, arrivals.at[number, i]) for i, (a, b) in enumerate(pairs)]
        )
        for copy in copies[-1]:
            copy.start()
    for number in range(parts):
        for copy in copies[number]:
            copy.wait()
        x = x_buffer[number]
        gate_part = jnp.dot(x, gate_buffer[number], preferred_element_type=jnp.float32)
        up_part = jnp.dot(x, up_buffer[number], preferred_element_type=jnp.float32)
        if number == 0:
            gate_sum[...] = gate_part
            up_sum[...] = up_part
        elif number < parts - 1:
            gate_sum[...] += gate_part
            up_sum[...] += up_part
        else:
            out_ref[...] = silu_times(gate_sum[...] + gate_part, up_sum[...] + up_part).astype(out_ref.dtype)


def hidden_units(me, xs, w_gate, w_up, after, told):
    gathered = len(xs) == 1
    parts, width, hidden = w_gate.shape
    rows = xs[0].shape[-2]
    return pl.pallas_call(
        functools.partial(hidden_kernel, gathered, parts),
        grid_spec=pltpu.PrefetchScalarGridSpec(
            num_scalar_prefetch=1,
            grid=(1,),
            in_specs=[IN_HBM] * (len(xs) + 2) + [CORNER] * len(after),
            out_specs=pl.BlockSpec((rows, hidden), lambda i, me: (0, 0)),
            scratch_shapes=[
                pltpu.VMEM((parts, rows, width), jnp.bfloat16),
                pltpu.VMEM((parts, width, hidden), jnp.bfloat16),
                pltpu.VMEM((parts, width, hidden), jnp.bfloat16),
                pltpu.VMEM((rows, hidden), jnp.float32),
                pltpu.VMEM((rows, hidden), jnp.float32),
                pltpu.SemaphoreType.DMA((parts, 4)),
            ],
        ),
        out_shape=jax.ShapeDtypeStruct((rows, hidden), jnp.bfloat16),
        compiler_params=pltpu.CompilerParams(vmem_limit_bytes=60 * MIB),
        cost_estimate=pl.CostEstimate(
            flops=4 * rows * parts * width * hidden * told,
            bytes_accessed=2 * parts * width * (rows + 2 * hidden) + 2 * rows * hidden,
            transcendentals=rows * hidden,
        ),
        name="hidden_units",
    )(me, *xs, w_gate, w_up, *after)


def down_kernel(parts, me_ref, *refs):
    acts, own_ref, pieces = refs[:parts], refs[parts], refs[parts + 1:2 * parts]
    out_ref, weights, slots, arrivals, departures = refs[-5:]
    width = slots.shape[2]
    tile = width // TILES
    copies = []
    for number in range(TILES):
        sources = [own_ref.at[:, pl.ds(pl.multiple_of(me_ref[0] * width + number * tile, 128), tile)]]
        sources += [piece.at[:, pl.ds(number * tile, tile)] for piece in pieces]
        copies.append([
            pltpu.make_async_copy(source, weights.at[number, i], arrivals.at[number, i])
            for i, source in enumerate(sources)
        ])
        for copy in copies[-1]:
            copy.start()
    leaving = []
    for number in range(TILES):
        for copy in copies[number]:
            copy.wait()
        total = jnp.dot(acts[0][...], weights[number, 0], preferred_element_type=jnp.float32)
        for i in range(1, parts):
            total += jnp.dot(acts[i][...], weights[number, i], preferred_element_type=jnp.float32)
        store_slots(slots.at[:, :, pl.ds(number * tile, tile)], total)
        where = pl.ds(number * tile, tile)
        leaving.append(
            pltpu.make_async_copy(slots.at[:, :, where], out_ref.at[:, :, where], departures.at[number])
        )
        leaving[-1].start()
    for copy in leaving:
        copy.wait()


def down(me, acts, w_down, pieces, experts):
    rows, hidden = acts[0].shape
    width = pieces[0].shape[1]
    parts = len(acts)
    shape = (experts, rows // experts, width)
    return pl.pallas_call(
        functools.partial(down_kernel, parts),
        grid_spec=pltpu.PrefetchScalarGridSpec(
            num_scalar_prefetch=1,
            grid=(1,),
            in_specs=[pl.BlockSpec((rows, hidden), lambda i, me: (0, 0))] * parts + [IN_HBM] * parts,
            out_specs=IN_HBM,
            scratch_shapes=[
                pltpu.VMEM((TILES, parts, hidden, width // TILES), jnp.bfloat16),
                pltpu.VMEM(shape, jnp.bfloat16),
                pltpu.SemaphoreType.DMA((TILES, parts)),
                pltpu.SemaphoreType.DMA((TILES,)),
            ],
        ),
        out_shape=jax.ShapeDtypeStruct(shape, jnp.bfloat16),
        compiler_params=pltpu.CompilerParams(vmem_limit_bytes=60 * MIB),
        cost_estimate=pl.CostEstimate(
            flops=2 * rows * parts * hidden * width,
            bytes_accessed=2 * (parts * hidden * (rows + width) + rows * width),
            transcendentals=0,
        ),
        name="down",
    )(me, *acts, w_down, *pieces)


def place_kernel(spot_ref, rows_ref, *rest):
    out_ref, slots, departures = rest[-3:]
    tile = rows_ref.shape[1] // TILES
    leaving = []
    for number in range(TILES):
        where = pl.ds(number * tile, tile)
        total = lax.dot_general(
            spot_ref[...], rows_ref[:, where], (((0,), (0,)), ((), ())), preferred_element_type=jnp.float32
        )
        store_slots(slots.at[:, :, where], total)
        leaving.append(
            pltpu.make_async_copy(slots.at[:, :, where], out_ref.at[:, :, where], departures.at[number])
        )
        leaving[-1].start()
    for copy in leaving:
        copy.wait()


def wait_kernel(*refs):
    refs[-1][...] = jnp.zeros(refs[-1].shape, refs[-1].dtype)


def wait_for(arrays, told):
    return pl.pallas_call(
        wait_kernel,
        grid=(1,),
        in_specs=[CORNER if array.ndim == 2 else CORNER_SLOTS for array in arrays],
        out_specs=CORNER,
        out_shape=jax.ShapeDtypeStruct((16, 128), jnp.bfloat16),
        cost_estimate=pl.CostEstimate(flops=told, bytes_accessed=0, transcendentals=0),
        name="wait_for",
    )(*arrays)


def place_rows(spot, rows, experts, after, told):
    slots, width = spot.shape[1], rows.shape[1]
    shape = (experts, slots // experts, width)
    return pl.pallas_call(
        place_kernel,
        grid=(1,),
        in_specs=[
            pl.BlockSpec((rows.shape[0], slots), lambda i: (0, 0)),
            pl.BlockSpec((rows.shape[0], width), lambda i: (0, 0)),
        ]
        + [CORNER if array.ndim == 2 else CORNER_SLOTS for array in after],
        out_specs=IN_HBM,
        scratch_shapes=[pltpu.VMEM(shape, jnp.bfloat16), pltpu.SemaphoreType.DMA((TILES,))],
        out_shape=jax.ShapeDtypeStruct(shape, jnp.bfloat16),
        compiler_params=pltpu.CompilerParams(vmem_limit_bytes=60 * MIB),
        cost_estimate=pl.CostEstimate(
            flops=2 * slots * rows.shape[0] * width * told,
            bytes_accessed=2 * (slots + rows.shape[0]) * width,
            transcendentals=0,
        ),
        name="place_rows",
    )(spot, rows, *after)


def on_device(hidden_rows, expert_ids, affinity, w_gate, w_up, w_down):
    experts = lax.axis_size("ep")
    parts = lax.axis_size("tp")
    row_count, width = hidden_rows.shape
    place = lax.axis_index("tp")
    me = place.reshape(1).astype(jnp.int32)
    w_gate = w_gate[0].reshape(parts, width, w_gate.shape[2])
    w_up = w_up[0].reshape(parts, width, w_up.shape[2])
    w_down = w_down[0]

    def send(array, step):
        return lax.ppermute(array, "tp", [(i, (i + step) % parts) for i in range(parts)])

    def send_all(array):
        return [send(array, step) for step in SENDS]

    def ring(rows):
        half = rows.shape[0] // 2
        left, right = send(rows, 1), send(rows, -1)
        return [left, right, send(left[:half], 1), send(right[half:], -1)]

    slices = [
        lax.dynamic_slice_in_dim(w_down, (place + step) % parts * width, width, axis=1) for step in SENDS
    ]
    pieces = [send(part, step) for part, step in zip(slices, SENDS)]

    route_weight = route_scale * affinity / jnp.sum(affinity, axis=1, keepdims=True)
    named = expert_ids[:, :, None] == jnp.arange(experts, dtype=jnp.int32)
    chosen = jnp.any(named, axis=1)
    weight = jnp.sum(jnp.where(named, route_weight[:, :, None], 0.0), axis=1)
    earlier = jnp.tril(jnp.ones((row_count, row_count), jnp.bfloat16), -1)
    slot = jnp.dot(earlier, chosen.astype(jnp.bfloat16), preferred_element_type=jnp.float32).astype(jnp.int32)
    slot = jnp.where(chosen, slot, CAP)

    places = []
    for first, count, _ in CHUNKS:
        here = slot[:, :, None] == first + jnp.arange(count, dtype=jnp.int32)
        places.append(here.reshape(row_count, experts * count))

    def outgoing(number, after):
        return place_rows(places[number].astype(jnp.bfloat16), hidden_rows, experts, after, 1)

    gathered = []
    leaving = [outgoing(0, []), None, None]
    leaving[2] = outgoing(2, leaving[:1])
    for number, (first, count, by_permutes) in enumerate(CHUNKS):
        if number == 1:
            leaving[1] = outgoing(1, [rows, leaving[2]])
        rows = lax.all_to_all(leaving[number], "ep", split_axis=0, concat_axis=0, tiled=True)
        rows = rows.reshape(experts * count, width)
        if number == 1:
            waited = wait_for([*pieces], WAIT_TOLD)
        if by_permutes:
            gathered.append([rows] + ring(rows))
        else:
            gathered.append([lax.all_gather(rows, "tp", tiled=True).reshape(parts, *rows.shape)])

    mixed = jnp.zeros((row_count, width), jnp.float32)
    for number, ((first, count, by_permutes), spot, x, told) in enumerate(zip(CHUNKS, places, gathered, TOLD)):
        after = [activated] if number else [waited]
        activated = hidden_units(me, x, w_gate, w_up, after, told)
        outputs = down(me, [activated] + send_all(activated), w_down, pieces, experts)
        returned = lax.all_to_all(outputs, "ep", split_axis=0, concat_axis=0, tiled=True)
        returned = returned.reshape(experts * count, width)
        mix = jnp.where(spot, jnp.repeat(weight, count, axis=1), 0.0)
        high = mix.astype(jnp.bfloat16)
        low = (mix - high.astype(jnp.float32)).astype(jnp.bfloat16)
        mixed = mixed + jnp.dot(high, returned, preferred_element_type=jnp.float32)
        mixed = mixed + jnp.dot(low, returned, preferred_element_type=jnp.float32)
    return mixed.astype(jnp.bfloat16)


def solution(mesh):
    in_specs = (
        P("ep", "tp"),
        P("ep", None),
        P("ep", None),
        P("ep", None, "tp"),
        P("ep", None, "tp"),
        P("ep", "tp", None),
    )
    out_specs = P("ep", "tp")
    return jax.shard_map(
        on_device, mesh=mesh, in_specs=in_specs, out_specs=out_specs, check_vma=False
    )
```

```python
import functools

import jax
import jax.numpy as jnp
from jax import lax
from jax.experimental import pallas as pl
from jax.experimental.pallas import tpu as pltpu
from jax.sharding import PartitionSpec as P

CAP = 12
CHUNKS = ((0, 4, 256), (4, 4, 256), (8, 4, 128))
SENDS = (1, 3, 2)
STEPS = (0, 3, 1, 2)
TILES = 2
TOLD = (1000, 100, 1)
WAIT_TOLD = 200_000_000_000
MIB = 1024 * 1024
CORNER = pl.BlockSpec((16, 128), lambda *index: (0, 0))
IN_HBM = pl.BlockSpec(memory_space=pltpu.HBM)
CORNER_SLOTS = pl.BlockSpec((8, 4, 128), lambda *index: (0, 0, 0))


route_scale = 2.5


def store_slots(out_ref, total):
    count = out_ref.shape[1]
    for expert in range(out_ref.shape[0]):
        out_ref[expert] = total[expert * count:(expert + 1) * count].astype(out_ref.dtype)


def silu_times(gate, up):
    return gate / (1.0 + jnp.exp(-gate)) * up


def hidden_kernel(gathered, parts, me_ref, *refs):
    pieces = 1 if gathered == refs[-7].shape[0] else parts + 1
    xs, (gate_ref, up_ref) = refs[:pieces], refs[pieces:pieces + 2]
    out_ref, x_buffer, gate_buffer, up_buffer, gate_sum, up_sum, arrivals = refs[-7:]
    rest = x_buffer.shape[1] - gathered
    copies = []
    for number, step in enumerate(STEPS):
        part = lax.rem(me_ref[0] + step, parts)
        pairs = [
            (gate_ref.at[part], gate_buffer.at[number]),
            (up_ref.at[part], up_buffer.at[number]),
            (xs[0].at[part], x_buffer.at[number, pl.ds(0, gathered)]),
        ]
        if rest:
            source = xs[1].at[pl.ds(gathered, rest)] if number == 0 else xs[1 + number]
            pairs.append((source, x_buffer.at[number, pl.ds(gathered, rest)]))
        copies.append(
            [pltpu.make_async_copy(a, b, arrivals.at[number, i]) for i, (a, b) in enumerate(pairs)]
        )
        for copy in copies[-1]:
            copy.start()
    for number in range(parts):
        for copy in copies[number]:
            copy.wait()
        x = x_buffer[number]
        gate_part = jnp.dot(x, gate_buffer[number], preferred_element_type=jnp.float32)
        up_part = jnp.dot(x, up_buffer[number], preferred_element_type=jnp.float32)
        if number == 0:
            gate_sum[...] = gate_part
            up_sum[...] = up_part
        elif number < parts - 1:
            gate_sum[...] += gate_part
            up_sum[...] += up_part
        else:
            out_ref[...] = silu_times(gate_sum[...] + gate_part, up_sum[...] + up_part).astype(out_ref.dtype)


def hidden_units(me, xs, w_gate, w_up, after, told):
    parts, width, hidden = w_gate.shape
    gathered = xs[0].shape[1]
    rows = gathered if len(xs) == 1 else xs[1].shape[0]
    return pl.pallas_call(
        functools.partial(hidden_kernel, gathered, parts),
        grid_spec=pltpu.PrefetchScalarGridSpec(
            num_scalar_prefetch=1,
            grid=(1,),
            in_specs=[IN_HBM] * (len(xs) + 2)
            + [CORNER if array.ndim == 2 else CORNER_SLOTS for array in after],
            out_specs=pl.BlockSpec((rows, hidden), lambda i, me: (0, 0)),
            scratch_shapes=[
                pltpu.VMEM((parts, rows, width), jnp.bfloat16),
                pltpu.VMEM((parts, width, hidden), jnp.bfloat16),
                pltpu.VMEM((parts, width, hidden), jnp.bfloat16),
                pltpu.VMEM((rows, hidden), jnp.float32),
                pltpu.VMEM((rows, hidden), jnp.float32),
                pltpu.SemaphoreType.DMA((parts, 4)),
            ],
        ),
        out_shape=jax.ShapeDtypeStruct((rows, hidden), jnp.bfloat16),
        compiler_params=pltpu.CompilerParams(vmem_limit_bytes=60 * MIB),
        cost_estimate=pl.CostEstimate(
            flops=4 * rows * parts * width * hidden * told,
            bytes_accessed=2 * parts * width * (rows + 2 * hidden) + 2 * rows * hidden,
            transcendentals=rows * hidden,
        ),
        name="hidden_units",
    )(me, *xs, w_gate, w_up, *after)


def down_kernel(parts, me_ref, *refs):
    acts, own_ref, pieces = refs[:parts], refs[parts], refs[parts + 1:2 * parts]
    out_ref, weights, slots, arrivals, departures = refs[-5:]
    width = slots.shape[2]
    tile = width // TILES
    copies = []
    for number in range(TILES):
        sources = [own_ref.at[:, pl.ds(pl.multiple_of(me_ref[0] * width + number * tile, 128), tile)]]
        sources += [piece.at[:, pl.ds(number * tile, tile)] for piece in pieces]
        copies.append([
            pltpu.make_async_copy(source, weights.at[number, i], arrivals.at[number, i])
            for i, source in enumerate(sources)
        ])
        for copy in copies[-1]:
            copy.start()
    leaving = []
    for number in range(TILES):
        for copy in copies[number]:
            copy.wait()
        total = jnp.dot(acts[0][...], weights[number, 0], preferred_element_type=jnp.float32)
        for i in range(1, parts):
            total += jnp.dot(acts[i][...], weights[number, i], preferred_element_type=jnp.float32)
        store_slots(slots.at[:, :, pl.ds(number * tile, tile)], total)
        where = pl.ds(number * tile, tile)
        leaving.append(
            pltpu.make_async_copy(slots.at[:, :, where], out_ref.at[:, :, where], departures.at[number])
        )
        leaving[-1].start()
    for copy in leaving:
        copy.wait()


def down(me, acts, w_down, pieces, experts):
    rows, hidden = acts[0].shape
    width = pieces[0].shape[1]
    parts = len(acts)
    shape = (experts, rows // experts, width)
    return pl.pallas_call(
        functools.partial(down_kernel, parts),
        grid_spec=pltpu.PrefetchScalarGridSpec(
            num_scalar_prefetch=1,
            grid=(1,),
            in_specs=[pl.BlockSpec((rows, hidden), lambda i, me: (0, 0))] * parts + [IN_HBM] * parts,
            out_specs=IN_HBM,
            scratch_shapes=[
                pltpu.VMEM((TILES, parts, hidden, width // TILES), jnp.bfloat16),
                pltpu.VMEM(shape, jnp.bfloat16),
                pltpu.SemaphoreType.DMA((TILES, parts)),
                pltpu.SemaphoreType.DMA((TILES,)),
            ],
        ),
        out_shape=jax.ShapeDtypeStruct(shape, jnp.bfloat16),
        compiler_params=pltpu.CompilerParams(vmem_limit_bytes=60 * MIB),
        cost_estimate=pl.CostEstimate(
            flops=2 * rows * parts * hidden * width,
            bytes_accessed=2 * (parts * hidden * (rows + width) + rows * width),
            transcendentals=0,
        ),
        name="down",
    )(me, *acts, w_down, *pieces)


def place_kernel(spot_ref, rows_ref, *rest):
    out_ref, slots, departures = rest[-3:]
    tile = rows_ref.shape[1] // TILES
    leaving = []
    for number in range(TILES):
        where = pl.ds(number * tile, tile)
        total = lax.dot_general(
            spot_ref[...], rows_ref[:, where], (((0,), (0,)), ((), ())), preferred_element_type=jnp.float32
        )
        store_slots(slots.at[:, :, where], total)
        leaving.append(
            pltpu.make_async_copy(slots.at[:, :, where], out_ref.at[:, :, where], departures.at[number])
        )
        leaving[-1].start()
    for copy in leaving:
        copy.wait()


def wait_kernel(*refs):
    refs[-1][...] = jnp.zeros(refs[-1].shape, refs[-1].dtype)


def wait_for(arrays, told):
    return pl.pallas_call(
        wait_kernel,
        grid=(1,),
        in_specs=[CORNER if array.ndim == 2 else CORNER_SLOTS for array in arrays],
        out_specs=CORNER,
        out_shape=jax.ShapeDtypeStruct((16, 128), jnp.bfloat16),
        cost_estimate=pl.CostEstimate(flops=told, bytes_accessed=0, transcendentals=0),
        name="wait_for",
    )(*arrays)


def place_rows(spot, rows, experts, after, told):
    slots, width = spot.shape[1], rows.shape[1]
    shape = (experts, slots // experts, width)
    return pl.pallas_call(
        place_kernel,
        grid=(1,),
        in_specs=[
            pl.BlockSpec((rows.shape[0], slots), lambda i: (0, 0)),
            pl.BlockSpec((rows.shape[0], width), lambda i: (0, 0)),
        ]
        + [CORNER if array.ndim == 2 else CORNER_SLOTS for array in after],
        out_specs=IN_HBM,
        scratch_shapes=[pltpu.VMEM(shape, jnp.bfloat16), pltpu.SemaphoreType.DMA((TILES,))],
        out_shape=jax.ShapeDtypeStruct(shape, jnp.bfloat16),
        compiler_params=pltpu.CompilerParams(vmem_limit_bytes=60 * MIB),
        cost_estimate=pl.CostEstimate(
            flops=2 * slots * rows.shape[0] * width * told,
            bytes_accessed=2 * (slots + rows.shape[0]) * width,
            transcendentals=0,
        ),
        name="place_rows",
    )(spot, rows, *after)


def on_device(hidden_rows, expert_ids, affinity, w_gate, w_up, w_down):
    experts = lax.axis_size("ep")
    parts = lax.axis_size("tp")
    row_count, width = hidden_rows.shape
    place = lax.axis_index("tp")
    me = place.reshape(1).astype(jnp.int32)
    w_gate = w_gate[0].reshape(parts, width, w_gate.shape[2])
    w_up = w_up[0].reshape(parts, width, w_up.shape[2])
    w_down = w_down[0]

    def send(array, step):
        return lax.ppermute(array, "tp", [(i, (i + step) % parts) for i in range(parts)])

    def send_all(array):
        return [send(array, step) for step in SENDS]

    slices = [
        lax.dynamic_slice_in_dim(w_down, (place + step) % parts * width, width, axis=1) for step in SENDS
    ]
    pieces = [send(part, step) for part, step in zip(slices, SENDS)]

    route_weight = route_scale * affinity / jnp.sum(affinity, axis=1, keepdims=True)
    named = expert_ids[:, :, None] == jnp.arange(experts, dtype=jnp.int32)
    chosen = jnp.any(named, axis=1)
    weight = jnp.sum(jnp.where(named, route_weight[:, :, None], 0.0), axis=1)
    earlier = jnp.tril(jnp.ones((row_count, row_count), jnp.bfloat16), -1)
    slot = jnp.dot(earlier, chosen.astype(jnp.bfloat16), preferred_element_type=jnp.float32).astype(jnp.int32)
    slot = jnp.where(chosen, slot, CAP)

    places = []
    for first, count, _ in CHUNKS:
        here = slot[:, :, None] == first + jnp.arange(count, dtype=jnp.int32)
        places.append(here.reshape(row_count, experts * count))

    def outgoing(number, after, told=1):
        return place_rows(places[number].astype(jnp.bfloat16), hidden_rows, experts, after, told)

    gathered = []
    leaving = [outgoing(0, []), None, None]
    for number, (first, count, by_gather) in enumerate(CHUNKS):
        if number == 1:
            leaving[1] = outgoing(1, [rows, *pieces[:2]], 3000)
        if number == 2:
            leaving[2] = outgoing(2, [rows])
        rows = lax.all_to_all(leaving[number], "ep", split_axis=0, concat_axis=0, tiled=True)
        rows = rows.reshape(experts * count, width)
        if number == 1:
            waited = wait_for([*pieces, rows], WAIT_TOLD)
        head = lax.all_gather(rows[:by_gather], "tp", tiled=True).reshape(parts, by_gather, width)
        gathered.append([head] + ([rows] + send_all(rows[by_gather:]) if by_gather < rows.shape[0] else []))

    mixed = jnp.zeros((row_count, width), jnp.float32)
    for number, ((first, count, _), spot, x, told) in enumerate(zip(CHUNKS, places, gathered, TOLD)):
        after = [outputs] if number else [waited]
        if number == 1:
            after = after + gathered[number + 1][2:]
        activated = hidden_units(me, x, w_gate, w_up, after, told)
        outputs = down(me, [activated] + send_all(activated), w_down, pieces, experts)
        returned = lax.all_to_all(outputs, "ep", split_axis=0, concat_axis=0, tiled=True)
        returned = returned.reshape(experts * count, width)
        mix = jnp.where(spot, jnp.repeat(weight, count, axis=1), 0.0)
        high = mix.astype(jnp.bfloat16)
        low = (mix - high.astype(jnp.float32)).astype(jnp.bfloat16)
        mixed = mixed + jnp.dot(high, returned, preferred_element_type=jnp.float32)
        mixed = mixed + jnp.dot(low, returned, preferred_element_type=jnp.float32)
    return mixed.astype(jnp.bfloat16)


def solution(mesh):
    in_specs = (
        P("ep", "tp"),
        P("ep", None),
        P("ep", None),
        P("ep", None, "tp"),
        P("ep", None, "tp"),
        P("ep", "tp", None),
    )
    out_specs = P("ep", "tp")
    return jax.shard_map(
        on_device, mesh=mesh, in_specs=in_specs, out_specs=out_specs, check_vma=False
    )
```

```python
import functools

import jax
import jax.numpy as jnp
from jax import lax
from jax.experimental import pallas as pl
from jax.experimental.pallas import tpu as pltpu
from jax.sharding import PartitionSpec as P

CAP = 12
DISPATCHES = ((0, 4), (4, 4), (8, 4))
CHUNKS = ((0, 4), (4, 4), (8, 2), (10, 2))
SENDS = (1, 3, 2)
TILES = 2
TOLD = (3000, 300, 30, 1)
WAIT_TOLD = 200_000_000_000
MIB = 1024 * 1024
CORNER = pl.BlockSpec((16, 128), lambda *index: (0, 0))
IN_HBM = pl.BlockSpec(memory_space=pltpu.HBM)


route_scale = 2.5


def corner(array):
    if array.ndim == 2:
        return CORNER
    return pl.BlockSpec((8, array.shape[1], 128), lambda *index: (0, 0, 0))


def store_slots(out_ref, total):
    count = out_ref.shape[1]
    for expert in range(out_ref.shape[0]):
        out_ref[expert] = total[expert * count:(expert + 1) * count].astype(out_ref.dtype)


def silu_times(gate, up):
    return gate / (1.0 + jnp.exp(-gate)) * up


def hidden_kernel(parts, me_ref, *refs):
    x_ref, gate_ref, up_ref = refs[:3]
    out_ref, x_buffer, gate_buffer, up_buffer, gate_sum, up_sum, arrivals = refs[-7:]
    copies = []
    for part in range(parts):
        pairs = (
            (gate_ref.at[part], gate_buffer.at[part]),
            (up_ref.at[part], up_buffer.at[part]),
            (x_ref.at[part], x_buffer.at[part]),
        )
        copies.append(
            [pltpu.make_async_copy(a, b, arrivals.at[part, i]) for i, (a, b) in enumerate(pairs)]
        )
        for copy in copies[-1]:
            copy.start()
    for number in range(parts):
        for copy in copies[number]:
            copy.wait()
        x = x_buffer[number]
        gate_part = jnp.dot(x, gate_buffer[number], preferred_element_type=jnp.float32)
        up_part = jnp.dot(x, up_buffer[number], preferred_element_type=jnp.float32)
        if number == 0:
            gate_sum[...] = gate_part
            up_sum[...] = up_part
        elif number < parts - 1:
            gate_sum[...] += gate_part
            up_sum[...] += up_part
        else:
            out_ref[...] = silu_times(gate_sum[...] + gate_part, up_sum[...] + up_part).astype(out_ref.dtype)


def hidden_units(me, x, w_gate, w_up, after, told):
    parts, rows, width = x.shape
    hidden = w_gate.shape[2]
    return pl.pallas_call(
        functools.partial(hidden_kernel, parts),
        grid_spec=pltpu.PrefetchScalarGridSpec(
            num_scalar_prefetch=1,
            grid=(1,),
            in_specs=[IN_HBM] * 3 + [corner(array) for array in after],
            out_specs=pl.BlockSpec((rows, hidden), lambda i, me: (0, 0)),
            scratch_shapes=[
                pltpu.VMEM((parts, rows, width), jnp.bfloat16),
                pltpu.VMEM((parts, width, hidden), jnp.bfloat16),
                pltpu.VMEM((parts, width, hidden), jnp.bfloat16),
                pltpu.VMEM((rows, hidden), jnp.float32),
                pltpu.VMEM((rows, hidden), jnp.float32),
                pltpu.SemaphoreType.DMA((parts, 3)),
            ],
        ),
        out_shape=jax.ShapeDtypeStruct((rows, hidden), jnp.bfloat16),
        compiler_params=pltpu.CompilerParams(vmem_limit_bytes=60 * MIB),
        cost_estimate=pl.CostEstimate(
            flops=4 * rows * parts * width * hidden * told,
            bytes_accessed=2 * parts * width * (rows + 2 * hidden) + 2 * rows * hidden,
            transcendentals=rows * hidden,
        ),
        name="hidden_units",
    )(me, x, w_gate, w_up, *after)


def down_kernel(parts, me_ref, *refs):
    acts, own_ref, pieces = refs[:parts], refs[parts], refs[parts + 1:2 * parts]
    out_ref, weights, slots, arrivals, departures = refs[-5:]
    width = slots.shape[2]
    tile = width // TILES
    copies = []
    for number in range(TILES):
        sources = [own_ref.at[:, pl.ds(pl.multiple_of(me_ref[0] * width + number * tile, 128), tile)]]
        sources += [piece.at[:, pl.ds(number * tile, tile)] for piece in pieces]
        copies.append([
            pltpu.make_async_copy(source, weights.at[number, i], arrivals.at[number, i])
            for i, source in enumerate(sources)
        ])
        for copy in copies[-1]:
            copy.start()
    leaving = []
    for number in range(TILES):
        for copy in copies[number]:
            copy.wait()
        total = jnp.dot(acts[0][...], weights[number, 0], preferred_element_type=jnp.float32)
        for i in range(1, parts):
            total += jnp.dot(acts[i][...], weights[number, i], preferred_element_type=jnp.float32)
        store_slots(slots.at[:, :, pl.ds(number * tile, tile)], total)
        where = pl.ds(number * tile, tile)
        leaving.append(
            pltpu.make_async_copy(slots.at[:, :, where], out_ref.at[:, :, where], departures.at[number])
        )
        leaving[-1].start()
    for copy in leaving:
        copy.wait()


def down(me, acts, w_down, pieces, experts):
    rows, hidden = acts[0].shape
    width = pieces[0].shape[1]
    parts = len(acts)
    shape = (experts, rows // experts, width)
    return pl.pallas_call(
        functools.partial(down_kernel, parts),
        grid_spec=pltpu.PrefetchScalarGridSpec(
            num_scalar_prefetch=1,
            grid=(1,),
            in_specs=[pl.BlockSpec((rows, hidden), lambda i, me: (0, 0))] * parts + [IN_HBM] * parts,
            out_specs=IN_HBM,
            scratch_shapes=[
                pltpu.VMEM((TILES, parts, hidden, width // TILES), jnp.bfloat16),
                pltpu.VMEM(shape, jnp.bfloat16),
                pltpu.SemaphoreType.DMA((TILES, parts)),
                pltpu.SemaphoreType.DMA((TILES,)),
            ],
        ),
        out_shape=jax.ShapeDtypeStruct(shape, jnp.bfloat16),
        compiler_params=pltpu.CompilerParams(vmem_limit_bytes=60 * MIB),
        cost_estimate=pl.CostEstimate(
            flops=2 * rows * parts * hidden * width,
            bytes_accessed=2 * (parts * hidden * (rows + width) + rows * width),
            transcendentals=0,
        ),
        name="down",
    )(me, *acts, w_down, *pieces)


def place_kernel(spot_ref, rows_ref, *rest):
    out_ref, slots, departures = rest[-3:]
    tile = rows_ref.shape[1] // TILES
    leaving = []
    for number in range(TILES):
        where = pl.ds(number * tile, tile)
        total = lax.dot_general(
            spot_ref[...], rows_ref[:, where], (((0,), (0,)), ((), ())), preferred_element_type=jnp.float32
        )
        store_slots(slots.at[:, :, where], total)
        leaving.append(
            pltpu.make_async_copy(slots.at[:, :, where], out_ref.at[:, :, where], departures.at[number])
        )
        leaving[-1].start()
    for copy in leaving:
        copy.wait()


def wait_kernel(*refs):
    refs[-1][...] = jnp.zeros(refs[-1].shape, refs[-1].dtype)


def wait_for(arrays, told):
    return pl.pallas_call(
        wait_kernel,
        grid=(1,),
        in_specs=[corner(array) for array in arrays],
        out_specs=CORNER,
        out_shape=jax.ShapeDtypeStruct((16, 128), jnp.bfloat16),
        cost_estimate=pl.CostEstimate(flops=told, bytes_accessed=0, transcendentals=0),
        name="wait_for",
    )(*arrays)


def place_rows(spot, rows, experts, after, told):
    slots, width = spot.shape[1], rows.shape[1]
    shape = (experts, slots // experts, width)
    return pl.pallas_call(
        place_kernel,
        grid=(1,),
        in_specs=[
            pl.BlockSpec((rows.shape[0], slots), lambda i: (0, 0)),
            pl.BlockSpec((rows.shape[0], width), lambda i: (0, 0)),
        ]
        + [corner(array) for array in after],
        out_specs=IN_HBM,
        scratch_shapes=[pltpu.VMEM(shape, jnp.bfloat16), pltpu.SemaphoreType.DMA((TILES,))],
        out_shape=jax.ShapeDtypeStruct(shape, jnp.bfloat16),
        compiler_params=pltpu.CompilerParams(vmem_limit_bytes=60 * MIB),
        cost_estimate=pl.CostEstimate(
            flops=2 * slots * rows.shape[0] * width * told,
            bytes_accessed=2 * (slots + rows.shape[0]) * width,
            transcendentals=0,
        ),
        name="place_rows",
    )(spot, rows, *after)


def on_device(hidden_rows, expert_ids, affinity, w_gate, w_up, w_down):
    experts = lax.axis_size("ep")
    parts = lax.axis_size("tp")
    row_count, width = hidden_rows.shape
    place = lax.axis_index("tp")
    me = place.reshape(1).astype(jnp.int32)
    w_gate = w_gate[0].reshape(parts, width, w_gate.shape[2])
    w_up = w_up[0].reshape(parts, width, w_up.shape[2])
    w_down = w_down[0]

    def send(array, step):
        return lax.ppermute(array, "tp", [(i, (i + step) % parts) for i in range(parts)])

    def send_all(array):
        return [send(array, step) for step in SENDS]

    slices = [
        lax.dynamic_slice_in_dim(w_down, (place + step) % parts * width, width, axis=1) for step in SENDS
    ]
    pieces = [send(part, step) for part, step in zip(slices, SENDS)]

    route_weight = route_scale * affinity / jnp.sum(affinity, axis=1, keepdims=True)
    named = expert_ids[:, :, None] == jnp.arange(experts, dtype=jnp.int32)
    chosen = jnp.any(named, axis=1)
    weight = jnp.sum(jnp.where(named, route_weight[:, :, None], 0.0), axis=1)
    earlier = jnp.tril(jnp.ones((row_count, row_count), jnp.bfloat16), -1)
    slot = jnp.dot(earlier, chosen.astype(jnp.bfloat16), preferred_element_type=jnp.float32).astype(jnp.int32)
    slot = jnp.where(chosen, slot, CAP)

    def spots(first, count):
        here = slot[:, :, None] == first + jnp.arange(count, dtype=jnp.int32)
        return here.reshape(row_count, experts * count)

    def outgoing(number, after):
        return place_rows(spots(*DISPATCHES[number]).astype(jnp.bfloat16), hidden_rows, experts, after, 1)

    gathered = []
    leaving = [outgoing(0, []), None, None]
    leaving[2] = outgoing(2, leaving[:1])
    for number, (first, count) in enumerate(DISPATCHES):
        if number == 1:
            leaving[1] = outgoing(1, [rows, leaving[2]])
        arrived = lax.all_to_all(leaving[number], "ep", split_axis=0, concat_axis=0, tiled=True)
        if number == 1:
            waited = wait_for([*pieces], WAIT_TOLD)
        for start, slots in CHUNKS:
            if first <= start < first + count:
                rows = arrived[:, start - first:start - first + slots].reshape(experts * slots, width)
                gathered.append(lax.all_gather(rows, "tp", tiled=True).reshape(parts, *rows.shape))

    back = []
    mixed = jnp.zeros((row_count, width), jnp.float32)
    for number, ((first, count), x, told) in enumerate(zip(CHUNKS, gathered, TOLD)):
        after = [outputs] + (back[number - 2:number - 1] if number > 1 else []) if number else [waited]
        activated = hidden_units(me, x, w_gate, w_up, after, told)
        outputs = down(me, [activated] + send_all(activated), w_down, pieces, experts)
        returned = lax.all_to_all(outputs, "ep", split_axis=0, concat_axis=0, tiled=True)
        back.append(returned)
        returned = returned.reshape(experts * count, width)
        mix = jnp.where(spots(first, count), jnp.repeat(weight, count, axis=1), 0.0)
        high = mix.astype(jnp.bfloat16)
        low = (mix - high.astype(jnp.float32)).astype(jnp.bfloat16)
        mixed = mixed + jnp.dot(high, returned, preferred_element_type=jnp.float32)
        mixed = mixed + jnp.dot(low, returned, preferred_element_type=jnp.float32)
    return mixed.astype(jnp.bfloat16)


def solution(mesh):
    in_specs = (
        P("ep", "tp"),
        P("ep", None),
        P("ep", None),
        P("ep", None, "tp"),
        P("ep", None, "tp"),
        P("ep", "tp", None),
    )
    out_specs = P("ep", "tp")
    return jax.shard_map(
        on_device, mesh=mesh, in_specs=in_specs, out_specs=out_specs, check_vma=False
    )
```

```python
import functools

import jax
import jax.numpy as jnp
from jax import lax
from jax.experimental import pallas as pl
from jax.experimental.pallas import tpu as pltpu
from jax.sharding import PartitionSpec as P

CAP = 12
CHUNKS = ((0, 4, False), (4, 4, False), (8, 4, False))
SENDS = (1, 3, 2)
STEPS = (0, 3, 1, 2)
TILES = 7
TOLD = (1000, 100, 1)
WAIT_TOLD = 200_000_000_000
MIB = 1024 * 1024
CORNER = pl.BlockSpec((16, 128), lambda *index: (0, 0))
IN_HBM = pl.BlockSpec(memory_space=pltpu.HBM)
CORNER_SLOTS = pl.BlockSpec((8, 4, 128), lambda *index: (0, 0, 0))


route_scale = 2.5


def store_slots(out_ref, total):
    count = out_ref.shape[1]
    for expert in range(out_ref.shape[0]):
        out_ref[expert] = total[expert * count:(expert + 1) * count].astype(out_ref.dtype)


def silu_times(gate, up):
    return gate / (1.0 + jnp.exp(-gate)) * up


def hidden_kernel(gathered, parts, me_ref, *refs):
    arrays = 1 if gathered else parts + 1
    xs, (gate_ref, up_ref) = refs[:arrays], refs[arrays:arrays + 2]
    out_ref, x_buffer, gate_buffer, up_buffer, gate_sum, up_sum, arrivals = refs[-7:]
    copies = []
    for number, step in enumerate(range(parts) if gathered else STEPS):
        part = step if gathered else lax.rem(me_ref[0] + step, parts)
        pairs = [(gate_ref.at[part], gate_buffer.at[number]), (up_ref.at[part], up_buffer.at[number])]
        if gathered:
            pairs.append((xs[0].at[step], x_buffer.at[number]))
        elif number < parts - 1:
            pairs.append((xs[number], x_buffer.at[number]))
        else:
            half = x_buffer.shape[1] // 2
            pairs.append((xs[number], x_buffer.at[number, pl.ds(0, half)]))
            pairs.append((xs[number + 1], x_buffer.at[number, pl.ds(half, half)]))
        copies.append(
            [pltpu.make_async_copy(a, b, arrivals.at[number, i]) for i, (a, b) in enumerate(pairs)]
        )
        for copy in copies[-1]:
            copy.start()
    for number in range(parts):
        for copy in copies[number]:
            copy.wait()
        x = x_buffer[number]
        gate_part = jnp.dot(x, gate_buffer[number], preferred_element_type=jnp.float32)
        up_part = jnp.dot(x, up_buffer[number], preferred_element_type=jnp.float32)
        if number == 0:
            gate_sum[...] = gate_part
            up_sum[...] = up_part
        elif number < parts - 1:
            gate_sum[...] += gate_part
            up_sum[...] += up_part
        else:
            out_ref[...] = silu_times(gate_sum[...] + gate_part, up_sum[...] + up_part).astype(out_ref.dtype)


def hidden_units(me, xs, w_gate, w_up, after, told):
    gathered = len(xs) == 1
    parts, width, hidden = w_gate.shape
    rows = xs[0].shape[-2]
    return pl.pallas_call(
        functools.partial(hidden_kernel, gathered, parts),
        grid_spec=pltpu.PrefetchScalarGridSpec(
            num_scalar_prefetch=1,
            grid=(1,),
            in_specs=[IN_HBM] * (len(xs) + 2) + [CORNER] * len(after),
            out_specs=pl.BlockSpec((rows, hidden), lambda i, me: (0, 0)),
            scratch_shapes=[
                pltpu.VMEM((parts, rows, width), jnp.bfloat16),
                pltpu.VMEM((parts, width, hidden), jnp.bfloat16),
                pltpu.VMEM((parts, width, hidden), jnp.bfloat16),
                pltpu.VMEM((rows, hidden), jnp.float32),
                pltpu.VMEM((rows, hidden), jnp.float32),
                pltpu.SemaphoreType.DMA((parts, 4)),
            ],
        ),
        out_shape=jax.ShapeDtypeStruct((rows, hidden), jnp.bfloat16),
        compiler_params=pltpu.CompilerParams(vmem_limit_bytes=60 * MIB),
        cost_estimate=pl.CostEstimate(
            flops=4 * rows * parts * width * hidden * told,
            bytes_accessed=2 * parts * width * (rows + 2 * hidden) + 2 * rows * hidden,
            transcendentals=rows * hidden,
        ),
        name="hidden_units",
    )(me, *xs, w_gate, w_up, *after)


def down_kernel(parts, me_ref, *refs):
    acts, own_ref, pieces = refs[:parts], refs[parts], refs[parts + 1:2 * parts]
    out_ref, weights, slots, arrivals, departures = refs[-5:]
    width = slots.shape[2]
    tile = width // TILES
    copies = []
    for number in range(TILES):
        sources = [own_ref.at[:, pl.ds(pl.multiple_of(me_ref[0] * width + number * tile, 128), tile)]]
        sources += [piece.at[:, pl.ds(number * tile, tile)] for piece in pieces]
        copies.append([
            pltpu.make_async_copy(source, weights.at[number, i], arrivals.at[number, i])
            for i, source in enumerate(sources)
        ])
        for copy in copies[-1]:
            copy.start()
    leaving = []
    for number in range(TILES):
        for copy in copies[number]:
            copy.wait()
        total = jnp.dot(acts[0][...], weights[number, 0], preferred_element_type=jnp.float32)
        for i in range(1, parts):
            total += jnp.dot(acts[i][...], weights[number, i], preferred_element_type=jnp.float32)
        store_slots(slots.at[:, :, pl.ds(number * tile, tile)], total)
        where = pl.ds(number * tile, tile)
        leaving.append(
            pltpu.make_async_copy(slots.at[:, :, where], out_ref.at[:, :, where], departures.at[number])
        )
        leaving[-1].start()
    for copy in leaving:
        copy.wait()


def down(me, acts, w_down, pieces, experts):
    rows, hidden = acts[0].shape
    width = pieces[0].shape[1]
    parts = len(acts)
    shape = (experts, rows // experts, width)
    return pl.pallas_call(
        functools.partial(down_kernel, parts),
        grid_spec=pltpu.PrefetchScalarGridSpec(
            num_scalar_prefetch=1,
            grid=(1,),
            in_specs=[pl.BlockSpec((rows, hidden), lambda i, me: (0, 0))] * parts + [IN_HBM] * parts,
            out_specs=IN_HBM,
            scratch_shapes=[
                pltpu.VMEM((TILES, parts, hidden, width // TILES), jnp.bfloat16),
                pltpu.VMEM(shape, jnp.bfloat16),
                pltpu.SemaphoreType.DMA((TILES, parts)),
                pltpu.SemaphoreType.DMA((TILES,)),
            ],
        ),
        out_shape=jax.ShapeDtypeStruct(shape, jnp.bfloat16),
        compiler_params=pltpu.CompilerParams(vmem_limit_bytes=60 * MIB),
        cost_estimate=pl.CostEstimate(
            flops=2 * rows * parts * hidden * width,
            bytes_accessed=2 * (parts * hidden * (rows + width) + rows * width),
            transcendentals=0,
        ),
        name="down",
    )(me, *acts, w_down, *pieces)


def place_kernel(spot_ref, rows_ref, *rest):
    out_ref, slots, departures = rest[-3:]
    tile = rows_ref.shape[1] // TILES
    leaving = []
    for number in range(TILES):
        where = pl.ds(number * tile, tile)
        total = lax.dot_general(
            spot_ref[...], rows_ref[:, where], (((0,), (0,)), ((), ())), preferred_element_type=jnp.float32
        )
        store_slots(slots.at[:, :, where], total)
        leaving.append(
            pltpu.make_async_copy(slots.at[:, :, where], out_ref.at[:, :, where], departures.at[number])
        )
        leaving[-1].start()
    for copy in leaving:
        copy.wait()


def wait_kernel(*refs):
    refs[-1][...] = jnp.zeros(refs[-1].shape, refs[-1].dtype)


def wait_for(arrays, told):
    return pl.pallas_call(
        wait_kernel,
        grid=(1,),
        in_specs=[CORNER if array.ndim == 2 else CORNER_SLOTS for array in arrays],
        out_specs=CORNER,
        out_shape=jax.ShapeDtypeStruct((16, 128), jnp.bfloat16),
        cost_estimate=pl.CostEstimate(flops=told, bytes_accessed=0, transcendentals=0),
        name="wait_for",
    )(*arrays)


def place_rows(spot, rows, experts, after, told):
    slots, width = spot.shape[1], rows.shape[1]
    shape = (experts, slots // experts, width)
    return pl.pallas_call(
        place_kernel,
        grid=(1,),
        in_specs=[
            pl.BlockSpec((rows.shape[0], slots), lambda i: (0, 0)),
            pl.BlockSpec((rows.shape[0], width), lambda i: (0, 0)),
        ]
        + [CORNER if array.ndim == 2 else CORNER_SLOTS for array in after],
        out_specs=IN_HBM,
        scratch_shapes=[pltpu.VMEM(shape, jnp.bfloat16), pltpu.SemaphoreType.DMA((TILES,))],
        out_shape=jax.ShapeDtypeStruct(shape, jnp.bfloat16),
        compiler_params=pltpu.CompilerParams(vmem_limit_bytes=60 * MIB),
        cost_estimate=pl.CostEstimate(
            flops=2 * slots * rows.shape[0] * width * told,
            bytes_accessed=2 * (slots + rows.shape[0]) * width,
            transcendentals=0,
        ),
        name="place_rows",
    )(spot, rows, *after)


def on_device(hidden_rows, expert_ids, affinity, w_gate, w_up, w_down):
    experts = lax.axis_size("ep")
    parts = lax.axis_size("tp")
    row_count, width = hidden_rows.shape
    place = lax.axis_index("tp")
    me = place.reshape(1).astype(jnp.int32)
    w_gate = w_gate[0].reshape(parts, width, w_gate.shape[2])
    w_up = w_up[0].reshape(parts, width, w_up.shape[2])
    w_down = w_down[0]

    def send(array, step):
        return lax.ppermute(array, "tp", [(i, (i + step) % parts) for i in range(parts)])

    def send_all(array):
        return [send(array, step) for step in SENDS]

    def ring(rows):
        half = rows.shape[0] // 2
        left, right = send(rows, 1), send(rows, -1)
        return [left, right, send(left[:half], 1), send(right[half:], -1)]

    slices = [
        lax.dynamic_slice_in_dim(w_down, (place + step) % parts * width, width, axis=1) for step in SENDS
    ]
    pieces = [send(part, step) for part, step in zip(slices, SENDS)]

    route_weight = route_scale * affinity / jnp.sum(affinity, axis=1, keepdims=True)
    named = expert_ids[:, :, None] == jnp.arange(experts, dtype=jnp.int32)
    chosen = jnp.any(named, axis=1)
    weight = jnp.sum(jnp.where(named, route_weight[:, :, None], 0.0), axis=1)
    earlier = jnp.tril(jnp.ones((row_count, row_count), jnp.bfloat16), -1)
    slot = jnp.dot(earlier, chosen.astype(jnp.bfloat16), preferred_element_type=jnp.float32).astype(jnp.int32)
    slot = jnp.where(chosen, slot, CAP)

    places = []
    for first, count, _ in CHUNKS:
        here = slot[:, :, None] == first + jnp.arange(count, dtype=jnp.int32)
        places.append(here.reshape(row_count, experts * count))

    def outgoing(number, after):
        return place_rows(places[number].astype(jnp.bfloat16), hidden_rows, experts, after, 1)

    gathered = []
    leaving = [outgoing(0, []), None, None]
    leaving[2] = outgoing(2, leaving[:1])
    for number, (first, count, by_permutes) in enumerate(CHUNKS):
        if number == 1:
            leaving[1] = outgoing(1, [rows, leaving[2]])
        rows = lax.all_to_all(leaving[number], "ep", split_axis=0, concat_axis=0, tiled=True)
        rows = rows.reshape(experts * count, width)
        if number == 1:
            waited = wait_for([*pieces], WAIT_TOLD)
        if by_permutes:
            gathered.append([rows] + ring(rows))
        else:
            gathered.append([lax.all_gather(rows, "tp", tiled=True).reshape(parts, *rows.shape)])

    mixed = jnp.zeros((row_count, width), jnp.float32)
    for number, ((first, count, by_permutes), spot, x, told) in enumerate(zip(CHUNKS, places, gathered, TOLD)):
        after = [activated] if number else [waited]
        activated = hidden_units(me, x, w_gate, w_up, after, told)
        outputs = down(me, [activated] + send_all(activated), w_down, pieces, experts)
        returned = lax.all_to_all(outputs, "ep", split_axis=0, concat_axis=0, tiled=True)
        returned = returned.reshape(experts * count, width)
        mix = jnp.where(spot, jnp.repeat(weight, count, axis=1), 0.0)
        high = mix.astype(jnp.bfloat16)
        low = (mix - high.astype(jnp.float32)).astype(jnp.bfloat16)
        mixed = mixed + jnp.dot(high, returned, preferred_element_type=jnp.float32)
        mixed = mixed + jnp.dot(low, returned, preferred_element_type=jnp.float32)
    return mixed.astype(jnp.bfloat16)


def solution(mesh):
    in_specs = (
        P("ep", "tp"),
        P("ep", None),
        P("ep", None),
        P("ep", None, "tp"),
        P("ep", None, "tp"),
        P("ep", "tp", None),
    )
    out_specs = P("ep", "tp")
    return jax.shard_map(
        on_device, mesh=mesh, in_specs=in_specs, out_specs=out_specs, check_vma=False
    )
```
